512 devices in a mesh: lat: 8 (over y, core), wave: 64 (over x, z).
Axes of the slice: x: 4, y: 4, z: 16, core: 2. Of those that a mesh axis runs over, the one named last changes fastest.
Arguments:
- grid_in: bfloat16 [1536, 64, 2560], P(('lat', 'wave')), may hold values from -6 to 6
- legendre: bfloat16 [640, 1536, 640], P('wave', 'lat'), may hold values from -0.15625 to 0.15625
- wave_order: int32 [640], replicated, may hold values from 0 to 639, as said below
- block_order: int32 [8], replicated, may hold values from 0 to 7, each once
- couple_div: float32 [32, 32], replicated, may hold values from -1 to 1
- couple_temp: float32 [32, 32], replicated, may hold values from -1 to 1
Outputs:
- spectral_out: bfloat16 [640, 640, 128], P('lat', 'wave')
- grid_out: bfloat16 [1536, 64, 2560], P(('lat', 'wave'))
The draws below stay inside these ranges and needn't reach their ends.
Inputs may be any that keep to these rules, and one draw needn't show every extreme that they name: `wave_order`: slots 2i and 2i+1 hold wavenumbers m and 639 - m for some m; every wavenumber stands in exactly one slot. `block_order`: each block index stands once.
All inputs are finite; a program needn't handle non-finite values.
Results may differ from the reference program's by a relative error of at most 0.0085.
Values may be sent and summed in bfloat16 or wider, within the bound.
No kernel may reach another device: no remote copies, remote signals or barrier semaphores. Data moves between devices by JAX's collectives and lax.ppermute only.
A program may use at most 64 MiB of HBM per device.

```python
import math
import jax
import jax.numpy as jnp
from jax import lax

NLAT = 1536
NLON = 2560
M = 640
F = 2
LEV = 32
NGROUPS = 8


def draw_wave_order(key, part):
    halves = M // 2
    shuffled = jax.random.permutation(jax.random.fold_in(key, 11), halves).astype(jnp.int32)
    flipped = jax.random.randint(jax.random.fold_in(key, 12), (halves,), 0, 2).astype(jnp.int32)
    leading = jnp.where(flipped == 1, M - 1 - shuffled, shuffled)
    trailing = M - 1 - leading
    return jnp.stack([leading, trailing], axis=1).reshape(M).astype(jnp.int32)


def block_levels(stream_key, shape, pieces, low, high):
    loudness = 1.0
    for dim, parts in pieces:
        steps = jax.random.uniform(jax.random.fold_in(jax.random.fold_in(stream_key, 6), dim), (parts,), jnp.float32, low / len(pieces), high / len(pieces))
        loudness = loudness * jnp.repeat(jnp.exp(steps), shape[dim] // parts).reshape((-1,) + (1,) * (len(shape) - 1 - dim))
    return loudness


def centred(stream_key, shape, width, reach, shards=(), kind=jnp.bfloat16):
    values = width * jax.random.normal(stream_key, shape, jnp.float32)
    if shards:
        values = values * block_levels(stream_key, shape, shards, -0.22, 0.18)
    return jnp.clip(values, -reach, reach).astype(kind)


def setup_inputs(seed: int = 0) -> dict:
    seeds = jax.random.split(jax.random.key(seed), 7)
    grid_in = centred(seeds[0], (NLAT, F * LEV, NLON), 1.0, 6.0, ((0, 512),))
    legendre = centred(seeds[1], (M, NLAT, M), NLAT ** -0.5, 0.15625, ((0, 64), (1, 8)))
    wave_order = draw_wave_order(jax.random.fold_in(seeds[6], 71), 0)
    block_order = jax.random.permutation(seeds[3], NGROUPS).astype(jnp.int32)
    couple_div = centred(seeds[4], (LEV, LEV), LEV ** -0.5, 1.0, (), jnp.float32)
    couple_temp = centred(seeds[5], (LEV, LEV), LEV ** -0.5, 1.0, (), jnp.float32)
    return {"grid_in": grid_in, "legendre": legendre, "wave_order": wave_order, "block_order": block_order, "couple_div": couple_div, "couple_temp": couple_temp}


def trig_table(wave_order, lon_width):
    columns = jnp.arange(lon_width, dtype=jnp.int32)
    phase_turns = columns[:, None] * wave_order[None, :] % lon_width
    angles = phase_turns.astype(jnp.float32) * (2.0 * math.pi / lon_width)
    factor = 1.0 / math.sqrt(lon_width)
    return jnp.stack([jnp.cos(angles) * factor, -jnp.sin(angles) * factor], axis=-1).astype(jnp.bfloat16)

def implicit(values, degrees, couple_div, couple_temp, levels, top_degree):
    shaped = values.reshape(values.shape[0], values.shape[1], 2, 2, levels)
    div_part = shaped[:, :, :, 0, :]
    temp_part = shaped[:, :, :, 1, :]
    factor = (degrees * (degrees + 1)).astype(jnp.float32) / float(top_degree * top_degree)
    pulled = jnp.einsum('nscq,pq->nscp', temp_part, couple_div, precision=lax.Precision.HIGHEST)
    pushed = jnp.einsum('nscq,pq->nscp', div_part, couple_temp, precision=lax.Precision.HIGHEST)
    new_div = div_part - factor[:, :, None, None] * pulled
    new_temp = temp_part - pushed
    return jnp.stack([new_div, new_temp], axis=3).reshape(values.shape).astype(jnp.bfloat16)

def forward_one(paired):
    columns, values = paired
    return jnp.dot(columns.T, values, preferred_element_type=jnp.float32)

def inverse_one(paired):
    columns, values = paired
    return jnp.dot(columns, values, preferred_element_type=jnp.float32).astype(jnp.bfloat16)

def reference(grid_in, legendre, wave_order, block_order, couple_div, couple_temp):
    trig = trig_table(wave_order, NLON)
    flattened = grid_in.reshape(NLAT * F * LEV, NLON)
    fourier = jnp.dot(flattened, trig.reshape(NLON, 2 * M), preferred_element_type=jnp.float32)
    fourier = fourier.reshape(NLAT, F * LEV, M, 2).transpose(0, 2, 3, 1).astype(jnp.bfloat16)
    fourier = fourier.reshape(NLAT, M, 2 * F * LEV)
    degrees = jnp.arange(M, dtype=jnp.int32)
    coeffs = lax.map(forward_one, (legendre, fourier.transpose(1, 0, 2)))
    keep_mask = degrees[None, :] >= wave_order[:, None]
    coeffs = jnp.where(keep_mask[:, :, None], coeffs, jnp.float32(0.0)).transpose(1, 0, 2)
    spectral = implicit(coeffs, degrees[:, None], couple_div, couple_temp, LEV, M)
    per_block = M // NGROUPS
    block_ids = jnp.take(block_order, degrees // per_block).astype(jnp.int32)
    spectral_out = jnp.take(spectral, block_ids * per_block + degrees % per_block, axis=0)
    returned = lax.map(inverse_one, (legendre, spectral.transpose(1, 0, 2)))
    weight = jnp.where(wave_order == 0, 1.0, 2.0).astype(jnp.bfloat16)
    weighted = trig * weight[None, :, None]
    lat_rows = returned.reshape(M, NLAT, 2, F * LEV).transpose(1, 3, 0, 2).reshape(NLAT * F * LEV, 2 * M)
    result = jnp.dot(lat_rows, weighted.reshape(NLON, 2 * M).T, preferred_element_type=jnp.float32)
    grid_out = result.reshape(NLAT, F * LEV, NLON).astype(jnp.bfloat16)
    return (spectral_out, grid_out)
```

```python
import functools
import math

import jax
import jax.numpy as jnp
from jax import lax
from jax.experimental import pallas as pl
from jax.experimental.pallas import tpu as pltpu
from jax.sharding import PartitionSpec as P

F32 = jnp.float32
BF16 = jnp.bfloat16
NLON = 2560
WAVES = 64
GROUPS = 8
SLOTS = 10
ROWS = 3
FIELDS = 64
K = 128
TOP = 640
BAND = 192
CHUNK = 32
UNIT = 16
UNITS = TOP // UNIT
PAIR_ROWS = TOP + UNIT
PACKED = 3328
SHARE = PACKED // GROUPS
VMEM_LIMIT = 56 * 1024 * 1024


def params():
    return pltpu.CompilerParams(
        dimension_semantics=("arbitrary",), vmem_limit_bytes=VMEM_LIMIT
    )


def cos_sin(phase):
    quarter = (
        (phase >= 320.0).astype(F32)
        + (phase >= 960.0).astype(F32)
        + (phase >= 1600.0).astype(F32)
        + (phase >= 2240.0).astype(F32)
    )
    x = (phase - 640.0 * quarter) * (2.0 * math.pi / NLON)
    y = x * x
    s = x * (
        1.0 + y * (-1.0 / 6 + y * (1.0 / 120 + y * (-1.0 / 5040 + y * (1.0 / 362880))))
    )
    c = 1.0 + y * (
        -0.5 + y * (1.0 / 24 + y * (-1.0 / 720 + y * (1.0 / 40320 + y * (-1.0 / 3628800))))
    )
    odd = (quarter == 1.0) | (quarter == 3.0)
    cos = jnp.where(odd, s, c)
    sin = jnp.where(odd, c, s)
    cos = jnp.where((quarter == 1.0) | (quarter == 2.0), -cos, cos)
    sin = jnp.where((quarter == 2.0) | (quarter == 3.0), -sin, sin)
    return cos, sin


def phase_of(product):
    return product - NLON * jnp.floor((product + 0.5) * (1.0 / NLON))


def forward_kernel(waves_ref, grid_ref, table_ref, send_ref, rows):
    step = pl.program_id(0)
    waves = waves_ref[...]
    lanes = lax.broadcasted_iota(jnp.int32, waves.shape, 1).astype(F32)
    near_c, near_s = cos_sin(phase_of(waves * lanes))
    far_c, far_s = cos_sin(phase_of(waves * (lanes * 128.0)))
    factor = 1.0 / math.sqrt(NLON)
    far_c = far_c * factor
    far_s = far_s * factor
    for a in range(NLON // 128):
        ca = far_c[:, a : a + 1]
        sa = far_s[:, a : a + 1]
        at = slice(a * 128, (a + 1) * 128)
        table_ref[0, :, at] = (ca * near_c - sa * near_s).astype(BF16)
        table_ref[1, :, at] = (-(sa * near_c) - ca * near_s).astype(BF16)
    table = table_ref[...].reshape(256, NLON)
    made = lax.dot_general(
        table, grid_ref[...], (((1,), (1,)), ((), ())), preferred_element_type=F32
    )
    for li in range(ROWS):
        at = slice(li * FIELDS, (li + 1) * FIELDS)
        both = jnp.concatenate([made[:128, at], made[128:, at]], axis=1)
        for q in range(2):
            row = (2 * step + q) * ROWS + li
            rows[pl.ds(row, WAVES, stride=CHUNK), :] = both[q * 64 : (q + 1) * 64]

    @pl.when(step == 4)
    def _():
        for row in range(SLOTS * ROWS, CHUNK):
            rows[pl.ds(row, WAVES, stride=CHUNK), :] = jnp.zeros((WAVES, K), F32)
        send_ref[...] = rows[...].astype(BF16)


def forward(waves, grid):
    return pl.pallas_call(
        forward_kernel,
        grid=(5,),
        in_specs=[
            pl.BlockSpec((128, 128), lambda i: (i, 0)),
            pl.BlockSpec((ROWS * FIELDS, NLON), lambda i: (0, 0)),
        ],
        out_specs=[
            pl.BlockSpec((2, 128, NLON), lambda i: (0, i, 0)),
            pl.BlockSpec((WAVES * CHUNK, K), lambda i: (0, 0)),
        ],
        out_shape=[
            jax.ShapeDtypeStruct((2, TOP, NLON), BF16),
            jax.ShapeDtypeStruct((WAVES * CHUNK, K), BF16),
        ],
        scratch_shapes=[pltpu.VMEM((WAVES * CHUNK, K), F32)],
        compiler_params=params(),
        cost_estimate=pl.CostEstimate(
            flops=2 * 192 * 2560 * 1280, bytes_accessed=9000000, transcendentals=0
        ),
        name="forward_rows",
    )(waves, grid)


def basis_kernel(own_ref, leg_ref, straight_ref, turned_ref, rows):
    wave = own_ref[pl.program_id(0)]
    for b in range(TOP // 128):
        at = slice(b * 128, (b + 1) * 128)
        rows[b] = leg_ref[0, :, at].astype(F32)
        for li in range(ROWS):
            straight_ref[0, li * WAVES : (li + 1) * WAVES, at] = rows[
                b, pl.ds(li, WAVES, stride=ROWS), :
            ].astype(BF16)
    turned = straight_ref[0].astype(F32).T
    degree = lax.broadcasted_iota(jnp.int32, turned.shape, 0)
    turned_ref[0] = jnp.where(degree >= wave, turned, 0.0).astype(BF16)


def basis(own, legendre):
    return pl.pallas_call(
        basis_kernel,
        grid=(SLOTS,),
        in_specs=[
            pl.BlockSpec(memory_space=pltpu.SMEM),
            pl.BlockSpec((1, BAND, TOP), lambda i: (i, 0, 0)),
        ],
        out_specs=[
            pl.BlockSpec((1, BAND, TOP), lambda i: (i, 0, 0)),
            pl.BlockSpec((1, TOP, BAND), lambda i: (i, 0, 0)),
        ],
        out_shape=[
            jax.ShapeDtypeStruct((SLOTS, BAND, TOP), BF16),
            jax.ShapeDtypeStruct((SLOTS, TOP, BAND), BF16),
        ],
        scratch_shapes=[pltpu.VMEM((TOP // 128, BAND, 128), F32)],
        compiler_params=params(),
        cost_estimate=pl.CostEstimate(
            flops=0, bytes_accessed=30000000, transcendentals=0
        ),
        name="basis_rows",
    )(own, legendre)


def partial_kernel(own_ref, turned_ref, got_ref, packed_ref, rows, tail):
    step = pl.program_id(0)

    @pl.when(step == 0)
    def _():
        rows[...] = got_ref[...].astype(F32)
        packed_ref[5 * PAIR_ROWS :, :] = jnp.zeros((PACKED - 5 * PAIR_ROWS, K), BF16)
        tail[TOP:, :] = jnp.zeros((TOP, K), F32)

    def product(q):
        slot = 2 * step + q
        values = jnp.concatenate(
            [
                rows[pl.ds(slot * ROWS + li, WAVES, stride=CHUNK), :]
                for li in range(ROWS)
            ],
            axis=0,
        ).astype(BF16)
        return jnp.dot(turned_ref[q], values, preferred_element_type=F32)

    unit = own_ref[2 * step] // UNIT
    tail[:TOP, :] = product(1)
    first = product(0)
    start = pl.multiple_of((UNITS - 1 - unit) * UNIT, UNIT)
    second = tail[pl.ds(start, PAIR_ROWS), :]
    first = jnp.concatenate([jnp.zeros((UNIT, K), F32), first], axis=0)
    row = lax.broadcasted_iota(jnp.int32, (PAIR_ROWS, K), 0)
    joined = jnp.where(row >= (unit + 1) * UNIT, first, second)
    at = pl.multiple_of(step * PAIR_ROWS, UNIT)
    packed_ref[pl.ds(at, PAIR_ROWS), :] = joined.astype(BF16)


def partial_sums(own, turned, got):
    return pl.pallas_call(
        partial_kernel,
        grid=(5,),
        in_specs=[
            pl.BlockSpec(memory_space=pltpu.SMEM),
            pl.BlockSpec((2, TOP, BAND), lambda i: (i, 0, 0)),
            pl.BlockSpec((WAVES * CHUNK, K), lambda i: (0, 0)),
        ],
        out_specs=pl.BlockSpec((PACKED, K), lambda i: (0, 0)),
        out_shape=jax.ShapeDtypeStruct((PACKED, K), BF16),
        scratch_shapes=[
            pltpu.VMEM((WAVES * CHUNK, K), F32),
            pltpu.VMEM((2 * TOP, K), F32),
        ],
        compiler_params=params(),
        cost_estimate=pl.CostEstimate(
            flops=2 * 10 * 192 * 640 * 128, bytes_accessed=5000000, transcendentals=0
        ),
        name="partial_sums",
    )(own, turned, got)


def couple_kernel(parts_ref, factor_ref, couple_ref, out_ref):
    total = parts_ref[0].astype(F32)
    for g in range(1, GROUPS):
        total = total + parts_ref[g].astype(F32)
    pulled = jnp.dot(
        total,
        couple_ref[...],
        preferred_element_type=F32,
        precision=lax.Precision.HIGHEST,
    )
    out_ref[...] = (total - factor_ref[...] * pulled).astype(BF16)


def couple(parts, factor, matrix):
    return pl.pallas_call(
        couple_kernel,
        out_shape=jax.ShapeDtypeStruct((SHARE, K), BF16),
        compiler_params=pltpu.CompilerParams(vmem_limit_bytes=VMEM_LIMIT),
        cost_estimate=pl.CostEstimate(
            flops=2 * 416 * 128 * 128 * 6, bytes_accessed=1200000, transcendentals=0
        ),
        name="couple_levels",
    )(parts, factor, matrix)


def inverse_kernel(own_ref, block_ref, straight_ref, all_ref, out_ref, send_ref, held, one, rows):
    step = pl.program_id(0)

    @pl.when(step == 0)
    def _():
        held[:TOP, :] = jnp.zeros((TOP, K), BF16)
        held[TOP:, :] = all_ref[...]

    unit = own_ref[2 * step] // UNIT
    row = lax.broadcasted_iota(jnp.int32, (TOP, K), 0)
    begin = block_ref[0] * (TOP // GROUPS)
    for q in range(2):
        if q == 0:
            start = TOP + step * PAIR_ROWS + UNIT
            least = unit * UNIT
        else:
            least = (UNITS - 1 - unit) * UNIT
            start = TOP + step * PAIR_ROWS - least
        start = pl.multiple_of(start, UNIT)
        values = held[pl.ds(start, TOP), :].astype(F32)
        one[q] = jnp.where(row >= least, values, 0.0).astype(BF16)
        out_ref[q] = one[q, pl.ds(pl.multiple_of(begin, UNIT), TOP // GROUPS), :]
        back = jnp.dot(straight_ref[q], one[q], preferred_element_type=F32)
        weight = jnp.where(own_ref[2 * step + q] == 0, 1.0, 2.0)
        back = back * weight
        for li in range(ROWS):
            at = (2 * step + q) * ROWS + li
            rows[pl.ds(at, WAVES, stride=CHUNK), :] = back[li * WAVES : (li + 1) * WAVES]

    @pl.when(step == 4)
    def _():
        for at in range(SLOTS * ROWS, CHUNK):
            rows[pl.ds(at, WAVES, stride=CHUNK), :] = jnp.zeros((WAVES, K), F32)
        send_ref[...] = rows[...].astype(BF16)


def inverse(own, block, straight, everything):
    return pl.pallas_call(
        inverse_kernel,
        grid=(5,),
        in_specs=[
            pl.BlockSpec(memory_space=pltpu.SMEM),
            pl.BlockSpec(memory_space=pltpu.SMEM),
            pl.BlockSpec((2, BAND, TOP), lambda i: (i, 0, 0)),
            pl.BlockSpec((PACKED, K), lambda i: (0, 0)),
        ],
        out_specs=[
            pl.BlockSpec((2, TOP // GROUPS, K), lambda i: (i, 0, 0)),
            pl.BlockSpec((WAVES * CHUNK, K), lambda i: (0, 0)),
        ],
        out_shape=[
            jax.ShapeDtypeStruct((SLOTS, TOP // GROUPS, K), BF16),
            jax.ShapeDtypeStruct((WAVES * CHUNK, K), BF16),
        ],
        scratch_shapes=[
            pltpu.VMEM((TOP + PACKED, K), BF16),
            pltpu.VMEM((2, TOP, K), BF16),
            pltpu.VMEM((WAVES * CHUNK, K), F32),
        ],
        compiler_params=params(),
        cost_estimate=pl.CostEstimate(
            flops=2 * 10 * 192 * 640 * 128, bytes_accessed=5000000, transcendentals=0
        ),
        name="inverse_sums",
    )(own, block, straight, everything)


def finish_kernel(got_ref, table_ref, out_ref, rows, left):
    @pl.when(pl.program_id(0) == 0)
    def _():
        rows[...] = got_ref[...].astype(F32)
        for li in range(ROWS):
            values = jnp.concatenate(
                [
                    rows[pl.ds(slot * ROWS + li, WAVES, stride=CHUNK), :]
                    for slot in range(SLOTS)
                ],
                axis=0,
            )
            turned = values.T.astype(BF16)
            at = slice(li * FIELDS, (li + 1) * FIELDS)
            left[at, :TOP] = turned[:FIELDS]
            left[at, TOP:] = turned[FIELDS:]

    table = table_ref[...].reshape(2 * TOP, table_ref.shape[2])
    out_ref[...] = jnp.dot(left[...], table, preferred_element_type=F32).astype(BF16)


def finish(got, table):
    block = 512
    return pl.pallas_call(
        finish_kernel,
        grid=(NLON // block,),
        in_specs=[
            pl.BlockSpec((WAVES * CHUNK, K), lambda i: (0, 0)),
            pl.BlockSpec((2, TOP, block), lambda i: (0, 0, i)),
        ],
        out_specs=pl.BlockSpec((ROWS * FIELDS, block), lambda i: (0, i)),
        out_shape=jax.ShapeDtypeStruct((ROWS * FIELDS, NLON), BF16),
        scratch_shapes=[
            pltpu.VMEM((WAVES * CHUNK, K), F32),
            pltpu.VMEM((ROWS * FIELDS, 2 * TOP), BF16),
        ],
        compiler_params=params(),
        cost_estimate=pl.CostEstimate(
            flops=2 * 192 * 2560 * 1280, bytes_accessed=9000000, transcendentals=0
        ),
        name="finish_rows",
    )(got, table)


def coupling_matrix(couple_div, couple_temp):
    zero = jnp.zeros_like(couple_div)
    one = jnp.block([[zero, couple_temp.T], [couple_div.T, zero]])
    none = jnp.zeros_like(one)
    return jnp.block([[one, none], [none, one]])


def packed_factor(own, offset):
    position = offset + lax.broadcasted_iota(jnp.int32, (SHARE, K), 0)
    column = lax.broadcasted_iota(jnp.int32, (SHARE, K), 1)
    pair = position // PAIR_ROWS
    inside = position - pair * PAIR_ROWS
    unit = jnp.zeros((SHARE, K), jnp.int32)
    for i in range(SLOTS // 2):
        unit = jnp.where(pair == i, own[2 * i] // UNIT, unit)
    degree = jnp.where(
        inside >= (unit + 1) * UNIT, inside - UNIT, inside + (UNITS - 1 - unit) * UNIT
    )
    factor = (degree * (degree + 1)).astype(F32) / float(TOP * TOP)
    return jnp.where(column % (K // 2) < K // 4, factor, 1.0)


def body(grid_in, legendre, wave_order, block_order, couple_div, couple_temp):
    lat = lax.axis_index("lat")
    wave = lax.axis_index("wave")
    own = lax.dynamic_slice_in_dim(wave_order, wave * SLOTS, SLOTS)
    block = lax.dynamic_slice_in_dim(block_order, lat, 1)
    waves = wave_order.reshape(WAVES, SLOTS).T.reshape(TOP, 1).astype(F32)
    waves = jnp.broadcast_to(waves, (TOP, 128))
    table, send = forward(waves, grid_in.reshape(ROWS * FIELDS, NLON))
    swap = functools.partial(lax.all_to_all, split_axis=0, concat_axis=0, tiled=True)
    got = swap(send.reshape(WAVES, CHUNK, K), "wave")
    straight, turned = basis(own, legendre)
    matrix = coupling_matrix(couple_div, couple_temp)
    factor = packed_factor(own, lat * SHARE)
    packed = partial_sums(own, turned, got.reshape(WAVES * CHUNK, K))
    parts = swap(packed.reshape(GROUPS, SHARE, K), "lat")
    spectral = couple(parts, factor, matrix)
    everything = lax.all_gather(spectral, "lat", axis=0, tiled=True)
    spectral_out, send = inverse(own, block, straight, everything)
    got = swap(send.reshape(WAVES, CHUNK, K), "wave")
    grid_out = finish(got.reshape(WAVES * CHUNK, K), table)
    return spectral_out.transpose(1, 0, 2), grid_out.reshape(ROWS, FIELDS, NLON)


def solution(mesh):
    placed = (P(("lat", "wave"), None, None), P("wave", "lat", None), P(), P(), P(), P())
    return jax.shard_map(
        body,
        mesh=mesh,
        in_specs=placed,
        out_specs=(P("lat", "wave", None), P(("lat", "wave"), None, None)),
        check_vma=False,
    )
```

```python
import functools
import math

import jax
import jax.numpy as jnp
from jax import lax
from jax.experimental import pallas as pl
from jax.experimental.pallas import tpu as pltpu
from jax.sharding import PartitionSpec as P

F32 = jnp.float32
BF16 = jnp.bfloat16
NLON = 2560
WAVES = 64
GROUPS = 8
SLOTS = 10
ROWS = 3
FIELDS = 64
K = 128
TOP = 640
BAND = 192
CHUNK = 32
UNIT = 16
UNITS = TOP // UNIT
PAIR_ROWS = TOP + UNIT
PACKED = 3328
SHARE = PACKED // GROUPS
VMEM_LIMIT = 24 * 1024 * 1024


def params():
    return pltpu.CompilerParams(
        dimension_semantics=("arbitrary",), vmem_limit_bytes=VMEM_LIMIT
    )


def cos_sin(phase):
    quarter = (
        (phase >= 320.0).astype(F32)
        + (phase >= 960.0).astype(F32)
        + (phase >= 1600.0).astype(F32)
        + (phase >= 2240.0).astype(F32)
    )
    x = (phase - 640.0 * quarter) * (2.0 * math.pi / NLON)
    y = x * x
    s = x * (
        1.0 + y * (-1.0 / 6 + y * (1.0 / 120 + y * (-1.0 / 5040 + y * (1.0 / 362880))))
    )
    c = 1.0 + y * (
        -0.5 + y * (1.0 / 24 + y * (-1.0 / 720 + y * (1.0 / 40320 + y * (-1.0 / 3628800))))
    )
    odd = (quarter == 1.0) | (quarter == 3.0)
    cos = jnp.where(odd, s, c)
    sin = jnp.where(odd, c, s)
    cos = jnp.where((quarter == 1.0) | (quarter == 2.0), -cos, cos)
    sin = jnp.where((quarter == 2.0) | (quarter == 3.0), -sin, sin)
    return cos, sin


def phase_of(product):
    return product - NLON * jnp.floor((product + 0.5) * (1.0 / NLON))


def forward_kernel(waves_ref, grid_ref, send_ref, table, lines, rows):
    step = pl.program_id(0)
    waves = waves_ref[...].astype(F32)
    down = lax.broadcasted_iota(jnp.int32, (128, 128), 0).astype(F32)
    near_c, near_s = cos_sin(phase_of(waves * down))
    far_c, far_s = cos_sin(phase_of(waves * (down[: NLON // 128 + 4] * 128.0)))
    factor = 1.0 / math.sqrt(NLON)
    far_c = far_c * factor
    far_s = far_s * factor
    for a in range(NLON // 128):
        ca = far_c[a : a + 1]
        sa = far_s[a : a + 1]
        at = slice(a * 128, (a + 1) * 128)
        table[at, :128] = (ca * near_c - sa * near_s).astype(BF16)
        table[at, 128:] = (-(sa * near_c) - ca * near_s).astype(BF16)
    made = jnp.dot(grid_ref[...], table[...], preferred_element_type=F32)
    at = pl.ds(pl.multiple_of(step * 128, 128), 128)
    for li in range(ROWS):
        one = made[li * FIELDS : (li + 1) * FIELDS]
        lines[li, at, :] = jnp.concatenate([one[:, :128], one[:, 128:]], axis=0).T

    @pl.when(step == 4)
    def _():
        for li in range(ROWS):
            for slot in range(SLOTS):
                rows[pl.ds(slot * ROWS + li, WAVES, stride=CHUNK), :] = lines[
                    li, pl.ds(slot, WAVES, stride=SLOTS), :
                ]
        for row in range(SLOTS * ROWS, CHUNK):
            rows[pl.ds(row, WAVES, stride=CHUNK), :] = jnp.zeros((WAVES, K), F32)
        send_ref[...] = rows[...].astype(BF16)


def forward(waves, grid):
    return pl.pallas_call(
        forward_kernel,
        grid=(5,),
        in_specs=[
            pl.BlockSpec((1, 128), lambda i: (0, i)),
            pl.BlockSpec((ROWS * FIELDS, NLON), lambda i: (0, 0)),
        ],
        out_specs=pl.BlockSpec((WAVES * CHUNK, K), lambda i: (0, 0)),
        out_shape=jax.ShapeDtypeStruct((WAVES * CHUNK, K), BF16),
        scratch_shapes=[
            pltpu.VMEM((NLON, 256), BF16),
            pltpu.VMEM((ROWS, TOP, K), F32),
            pltpu.VMEM((WAVES * CHUNK, K), F32),
        ],
        compiler_params=params(),
        cost_estimate=pl.CostEstimate(
            flops=2 * 192 * 2560 * 1280, bytes_accessed=2000000, transcendentals=0
        ),
        name="forward_rows",
    )(waves, grid)


def table_kernel(waves_ref, table_ref):
    waves = waves_ref[...]
    lanes = lax.broadcasted_iota(jnp.int32, waves.shape, 1).astype(F32)
    near_c, near_s = cos_sin(phase_of(waves * lanes))
    far_c, far_s = cos_sin(phase_of(waves * (lanes * 128.0)))
    factor = 1.0 / math.sqrt(NLON)
    far_c = far_c * factor
    far_s = far_s * factor
    for a in range(NLON // 128):
        ca = far_c[:, a : a + 1]
        sa = far_s[:, a : a + 1]
        at = slice(a * 128, (a + 1) * 128)
        table_ref[0, :, at] = (ca * near_c - sa * near_s).astype(BF16)
        table_ref[1, :, at] = (-(sa * near_c) - ca * near_s).astype(BF16)


def inverse_table(waves):
    return pl.pallas_call(
        table_kernel,
        grid=(5,),
        in_specs=[pl.BlockSpec((128, 128), lambda i: (i, 0))],
        out_specs=pl.BlockSpec((2, 128, NLON), lambda i: (0, i, 0)),
        out_shape=jax.ShapeDtypeStruct((2, TOP, NLON), BF16),
        compiler_params=params(),
        cost_estimate=pl.CostEstimate(
            flops=30000000, bytes_accessed=12000000, transcendentals=0
        ),
        name="inverse_table",
    )(waves)


def basis_kernel(own_ref, leg_ref, straight_ref, turned_ref, rows, joined):
    wave = own_ref[pl.program_id(0)]
    for b in range(TOP // 128):
        at = slice(b * 128, (b + 1) * 128)
        degree = b * 128 + lax.broadcasted_iota(jnp.int32, (BAND, 128), 1)
        rows[b] = jnp.where(degree >= wave, leg_ref[0, :, at].astype(F32), 0.0)
        for li in range(ROWS):
            joined[li * WAVES : (li + 1) * WAVES, at] = rows[
                b, pl.ds(li, WAVES, stride=ROWS), :
            ]
    straight_ref[0] = joined[...].astype(BF16)
    turned_ref[0] = joined[...].T.astype(BF16)


def basis(own, legendre):
    return pl.pallas_call(
        basis_kernel,
        grid=(SLOTS,),
        in_specs=[
            pl.BlockSpec(memory_space=pltpu.SMEM),
            pl.BlockSpec((1, BAND, TOP), lambda i: (i, 0, 0)),
        ],
        out_specs=[
            pl.BlockSpec((1, BAND, TOP), lambda i: (i, 0, 0)),
            pl.BlockSpec((1, TOP, BAND), lambda i: (i, 0, 0)),
        ],
        out_shape=[
            jax.ShapeDtypeStruct((SLOTS, BAND, TOP), BF16),
            jax.ShapeDtypeStruct((SLOTS, TOP, BAND), BF16),
        ],
        scratch_shapes=[
            pltpu.VMEM((TOP // 128, BAND, 128), F32),
            pltpu.VMEM((BAND, TOP), F32),
        ],
        compiler_params=params(),
        cost_estimate=pl.CostEstimate(
            flops=0, bytes_accessed=30000000, transcendentals=0
        ),
        name="basis_rows",
    )(own, legendre)


def partial_kernel(own_ref, turned_ref, got_ref, packed_ref, rows, held):
    step = pl.program_id(0)
    pair = 4 - step

    @pl.when(step == 0)
    def _():
        rows[...] = got_ref[...].astype(F32)
        held[TOP + 5 * PAIR_ROWS :, :] = jnp.zeros((PACKED - 5 * PAIR_ROWS, K), BF16)

    def product(q):
        slot = 2 * pair + q
        values = jnp.concatenate(
            [
                rows[pl.ds(slot * ROWS + li, WAVES, stride=CHUNK), :]
                for li in range(ROWS)
            ],
            axis=0,
        ).astype(BF16)
        return jnp.dot(turned_ref[q], values, preferred_element_type=F32).astype(BF16)

    unit = own_ref[2 * pair] // UNIT
    base = TOP + pair * PAIR_ROWS
    held[pl.ds(pl.multiple_of(base + UNIT, UNIT), TOP), :] = product(0)
    at = pl.multiple_of(base - (UNITS - 1 - unit) * UNIT, UNIT)
    held[pl.ds(at, TOP), :] = product(1)

    @pl.when(step == 4)
    def _():
        packed_ref[...] = held[TOP:, :]


def partial_sums(own, turned, got):
    return pl.pallas_call(
        partial_kernel,
        grid=(5,),
        in_specs=[
            pl.BlockSpec(memory_space=pltpu.SMEM),
            pl.BlockSpec((2, TOP, BAND), lambda i: (4 - i, 0, 0)),
            pl.BlockSpec((WAVES * CHUNK, K), lambda i: (0, 0)),
        ],
        out_specs=pl.BlockSpec((PACKED, K), lambda i: (0, 0)),
        out_shape=jax.ShapeDtypeStruct((PACKED, K), BF16),
        scratch_shapes=[
            pltpu.VMEM((WAVES * CHUNK, K), F32),
            pltpu.VMEM((TOP + PACKED, K), BF16),
        ],
        compiler_params=params(),
        cost_estimate=pl.CostEstimate(
            flops=2 * 10 * 192 * 640 * 128, bytes_accessed=5000000, transcendentals=0
        ),
        name="partial_sums",
    )(own, turned, got)


def couple_kernel(own_ref, lat_ref, parts_ref, couple_ref, out_ref):
    total = parts_ref[0].astype(F32)
    for g in range(1, GROUPS):
        total = total + parts_ref[g].astype(F32)
    pulled = jnp.dot(
        total,
        couple_ref[...],
        preferred_element_type=F32,
        precision=lax.Precision.HIGHEST,
    )
    position = lat_ref[0] * SHARE + lax.broadcasted_iota(jnp.int32, (SHARE, K), 0)
    degree = jnp.zeros((SHARE, K), jnp.int32)
    for pair in range(SLOTS // 2):
        unit = own_ref[2 * pair] // UNIT
        inside = position - pair * PAIR_ROWS
        shift = jnp.where(inside >= (unit + 1) * UNIT, -UNIT, (UNITS - 1 - unit) * UNIT)
        degree = jnp.where(inside >= 0, inside + shift, degree)
    degree = degree.astype(F32)
    column = lax.broadcasted_iota(jnp.int32, (SHARE, K), 1)
    factor = jnp.where(
        (column & 63) < 32, degree * (degree + 1.0) / float(TOP * TOP), 1.0
    )
    out_ref[...] = (total - factor * pulled).astype(BF16)


def couple(own, lat, parts, matrix):
    return pl.pallas_call(
        couple_kernel,
        in_specs=[
            pl.BlockSpec(memory_space=pltpu.SMEM),
            pl.BlockSpec(memory_space=pltpu.SMEM),
            pl.BlockSpec(memory_space=pltpu.VMEM),
            pl.BlockSpec(memory_space=pltpu.VMEM),
        ],
        out_specs=pl.BlockSpec(memory_space=pltpu.VMEM),
        out_shape=jax.ShapeDtypeStruct((SHARE, K), BF16),
        compiler_params=pltpu.CompilerParams(vmem_limit_bytes=VMEM_LIMIT),
        cost_estimate=pl.CostEstimate(
            flops=2 * 416 * 128 * 128 * 6, bytes_accessed=1200000, transcendentals=0
        ),
        name="couple_levels",
    )(own, lat, parts, matrix)


def inverse_kernel(own_ref, block_ref, straight_ref, all_ref, out_ref, send_ref, held, rows):
    step = pl.program_id(0)

    @pl.when(step == 0)
    def _():
        held[:TOP, :] = jnp.zeros((TOP, K), BF16)
        held[TOP:, :] = all_ref[...]

    base = TOP + step * PAIR_ROWS
    unit = own_ref[2 * step] // UNIT
    size = TOP // GROUPS
    begin = block_ref[0] * size
    degree = begin + lax.broadcasted_iota(jnp.int32, (size, K), 0)
    for q in range(2):
        wave = own_ref[2 * step + q]
        start = base + UNIT if q == 0 else base - (UNITS - 1 - unit) * UNIT
        values = held[pl.ds(pl.multiple_of(start, UNIT), TOP), :]
        back = jnp.dot(straight_ref[q], values, preferred_element_type=F32)
        back = back * jnp.where(wave == 0, 1.0, 2.0)
        for li in range(ROWS):
            at = (2 * step + q) * ROWS + li
            rows[pl.ds(at, WAVES, stride=CHUNK), :] = back[li * WAVES : (li + 1) * WAVES]
        mine = held[pl.ds(pl.multiple_of(start + begin, UNIT), size), :]
        out_ref[q] = jnp.where(degree >= wave, mine.astype(F32), 0.0).astype(BF16)

    @pl.when(step == 4)
    def _():
        for at in range(SLOTS * ROWS, CHUNK):
            rows[pl.ds(at, WAVES, stride=CHUNK), :] = jnp.zeros((WAVES, K), F32)
        send_ref[...] = rows[...].astype(BF16)


def inverse(own, block, straight, everything):
    return pl.pallas_call(
        inverse_kernel,
        grid=(5,),
        in_specs=[
            pl.BlockSpec(memory_space=pltpu.SMEM),
            pl.BlockSpec(memory_space=pltpu.SMEM),
            pl.BlockSpec((2, BAND, TOP), lambda i: (i, 0, 0)),
            pl.BlockSpec((PACKED, K), lambda i: (0, 0)),
        ],
        out_specs=[
            pl.BlockSpec((2, TOP // GROUPS, K), lambda i: (i, 0, 0)),
            pl.BlockSpec((WAVES * CHUNK, K), lambda i: (0, 0)),
        ],
        out_shape=[
            jax.ShapeDtypeStruct((SLOTS, TOP // GROUPS, K), BF16),
            jax.ShapeDtypeStruct((WAVES * CHUNK, K), BF16),
        ],
        scratch_shapes=[
            pltpu.VMEM((TOP + PACKED, K), BF16),
            pltpu.VMEM((WAVES * CHUNK, K), F32),
        ],
        compiler_params=params(),
        cost_estimate=pl.CostEstimate(
            flops=2 * 10 * 192 * 640 * 128, bytes_accessed=5000000, transcendentals=0
        ),
        name="inverse_sums",
    )(own, block, straight, everything)


def finish_kernel(got_ref, table_ref, out_ref, rows, left):
    @pl.when(pl.program_id(0) == 0)
    def _():
        rows[...] = got_ref[...].astype(F32)
        for li in range(ROWS):
            values = jnp.concatenate(
                [
                    rows[pl.ds(slot * ROWS + li, WAVES, stride=CHUNK), :]
                    for slot in range(SLOTS)
                ],
                axis=0,
            )
            turned = values.T.astype(BF16)
            at = slice(li * FIELDS, (li + 1) * FIELDS)
            left[at, :TOP] = turned[:FIELDS]
            left[at, TOP:] = turned[FIELDS:]

    table = table_ref[...].reshape(2 * TOP, table_ref.shape[2])
    out_ref[...] = jnp.dot(left[...], table, preferred_element_type=F32).astype(BF16)


def finish(got, table):
    block = 512
    return pl.pallas_call(
        finish_kernel,
        grid=(NLON // block,),
        in_specs=[
            pl.BlockSpec((WAVES * CHUNK, K), lambda i: (0, 0)),
            pl.BlockSpec((2, TOP, block), lambda i: (0, 0, i)),
        ],
        out_specs=pl.BlockSpec((ROWS * FIELDS, block), lambda i: (0, i)),
        out_shape=jax.ShapeDtypeStruct((ROWS * FIELDS, NLON), BF16),
        scratch_shapes=[
            pltpu.VMEM((WAVES * CHUNK, K), F32),
            pltpu.VMEM((ROWS * FIELDS, 2 * TOP), BF16),
        ],
        compiler_params=params(),
        cost_estimate=pl.CostEstimate(
            flops=2 * 192 * 2560 * 1280, bytes_accessed=9000000, transcendentals=0
        ),
        name="finish_rows",
    )(got, table)


def coupling_matrix(couple_div, couple_temp):
    zero = jnp.zeros_like(couple_div)
    one = jnp.block([[zero, couple_temp.T], [couple_div.T, zero]])
    none = jnp.zeros_like(one)
    return jnp.block([[one, none], [none, one]])


def body(grid_in, legendre, wave_order, block_order, couple_div, couple_temp):
    lat = lax.axis_index("lat")
    wave = lax.axis_index("wave")
    send = forward(wave_order.reshape(1, TOP), grid_in.reshape(ROWS * FIELDS, NLON))
    swap = functools.partial(lax.all_to_all, split_axis=0, concat_axis=0, tiled=True)
    got = swap(send.reshape(WAVES, CHUNK, K), "wave")
    own = lax.dynamic_slice_in_dim(wave_order, wave * SLOTS, SLOTS)
    block = lax.dynamic_slice_in_dim(block_order, lat, 1)
    straight, turned = basis(own, legendre)
    waves = wave_order.reshape(WAVES, SLOTS).T.reshape(TOP, 1).astype(F32)
    table = inverse_table(jnp.broadcast_to(waves, (TOP, 128)))
    matrix = coupling_matrix(couple_div, couple_temp)
    packed = partial_sums(own, turned, got.reshape(WAVES * CHUNK, K))
    parts = swap(packed.reshape(GROUPS, SHARE, K), "lat")
    spectral = couple(own, lat.reshape(1), parts, matrix)
    everything = lax.all_gather(spectral, "lat", axis=0, tiled=True)
    spectral_out, send = inverse(own, block, straight, everything)
    got = swap(send.reshape(WAVES, CHUNK, K), "wave")
    grid_out = finish(got.reshape(WAVES * CHUNK, K), table)
    return spectral_out.transpose(1, 0, 2), grid_out.reshape(ROWS, FIELDS, NLON)


def solution(mesh):
    placed = (P(("lat", "wave"), None, None), P("wave", "lat", None), P(), P(), P(), P())
    return jax.shard_map(
        body,
        mesh=mesh,
        in_specs=placed,
        out_specs=(P("lat", "wave", None), P(("lat", "wave"), None, None)),
        check_vma=False,
    )
```

```python
import functools
import math

import jax
import jax.numpy as jnp
from jax import lax
from jax.experimental import pallas as pl
from jax.experimental.pallas import tpu as pltpu
from jax.sharding import PartitionSpec as P

F32 = jnp.float32
BF16 = jnp.bfloat16
NLON = 2560
WAVES = 64
GROUPS = 8
SLOTS = 10
ROWS = 3
FIELDS = 64
K = 128
TOP = 640
BAND = 192
CHUNK = 32
UNIT = 16
UNITS = TOP // UNIT
PAIR_ROWS = TOP + UNIT
PACKED = 3328
SHARE = PACKED // GROUPS
VMEM_LIMIT = 24 * 1024 * 1024
LARGE = 58 * 1024 * 1024
MIDDLE = 50 * 1024 * 1024


def params(limit=VMEM_LIMIT):
    return pltpu.CompilerParams(
        dimension_semantics=("arbitrary",), vmem_limit_bytes=limit
    )


def cos_sin(phase):
    quarter = (
        (phase >= 320.0).astype(F32)
        + (phase >= 960.0).astype(F32)
        + (phase >= 1600.0).astype(F32)
        + (phase >= 2240.0).astype(F32)
    )
    x = (phase - 640.0 * quarter) * (2.0 * math.pi / NLON)
    y = x * x
    s = x * (
        1.0 + y * (-1.0 / 6 + y * (1.0 / 120 + y * (-1.0 / 5040 + y * (1.0 / 362880))))
    )
    c = 1.0 + y * (
        -0.5 + y * (1.0 / 24 + y * (-1.0 / 720 + y * (1.0 / 40320 + y * (-1.0 / 3628800))))
    )
    odd = (quarter == 1.0) | (quarter == 3.0)
    cos = jnp.where(odd, s, c)
    sin = jnp.where(odd, c, s)
    cos = jnp.where((quarter == 1.0) | (quarter == 2.0), -cos, cos)
    sin = jnp.where((quarter == 2.0) | (quarter == 3.0), -sin, sin)
    return cos, sin


def phase_of(product):
    return product - NLON * jnp.floor((product + 0.5) * (1.0 / NLON))


def forward_kernel(waves_ref, grid_ref, send_ref, grid, table, lines, rows, sem):
    load = pltpu.make_async_copy(grid_ref, grid, sem)
    load.start()
    factor = 1.0 / math.sqrt(NLON)
    half = NLON // 2
    for step in range(TOP // 128):
        waves = waves_ref[step * 128 : (step + 1) * 128].astype(F32).reshape(1, 128)
        down = lax.broadcasted_iota(jnp.int32, (128, 128), 0).astype(F32)
        near_c, near_s = cos_sin(phase_of(waves * down))
        far_c, far_s = cos_sin(phase_of(waves * (down[:16] * 128.0)))
        far_c = far_c * factor
        far_s = far_s * factor
        sign = 1.0 - 2.0 * (waves - 2.0 * jnp.floor(waves * 0.5))
        held = table.at[step % 2]
        for a in range(half // 128):
            ca = far_c[a : a + 1]
            sa = far_s[a : a + 1]
            c = ca * near_c - sa * near_s
            s = -(sa * near_c) - ca * near_s
            at = slice(a * 128, (a + 1) * 128)
            held[at, :128] = c.astype(BF16)
            held[at, 128:] = s.astype(BF16)
            at = slice(half + a * 128, half + (a + 1) * 128)
            held[at, :128] = (c * sign).astype(BF16)
            held[at, 128:] = (s * sign).astype(BF16)
        if step == 0:
            load.wait()
        made = jnp.dot(grid[...], held[...], preferred_element_type=F32)
        at = slice(step * 128, (step + 1) * 128)
        for li in range(ROWS):
            one = made[li * FIELDS : (li + 1) * FIELDS]
            lines[li, at, :] = jnp.concatenate([one[:, :128], one[:, 128:]], axis=0).T
    for li in range(ROWS):
        for slot in range(SLOTS):
            rows[pl.ds(slot * ROWS + li, WAVES, stride=CHUNK), :] = lines[
                li, pl.ds(slot, WAVES, stride=SLOTS), :
            ]
    clear_spare(rows)
    send_ref[...] = rows[...].astype(BF16)


def clear_spare(rows):
    for row in range(SLOTS * ROWS, CHUNK):
        rows[pl.ds(row, WAVES, stride=CHUNK), :] = jnp.zeros((WAVES, K), F32)


def forward(waves, grid):
    return pl.pallas_call(
        forward_kernel,
        in_specs=[
            pl.BlockSpec(memory_space=pltpu.VMEM),
            pl.BlockSpec(memory_space=pl.ANY),
        ],
        out_specs=pl.BlockSpec(memory_space=pltpu.VMEM),
        out_shape=jax.ShapeDtypeStruct((WAVES * CHUNK, K), BF16),
        scratch_shapes=[
            pltpu.VMEM((ROWS * FIELDS, NLON), BF16),
            pltpu.VMEM((2, NLON, 256), BF16),
            pltpu.VMEM((ROWS, TOP, K), F32),
            pltpu.VMEM((WAVES * CHUNK, K), F32),
            pltpu.SemaphoreType.DMA,
        ],
        compiler_params=pltpu.CompilerParams(vmem_limit_bytes=LARGE),
        cost_estimate=pl.CostEstimate(
            flops=2 * 192 * 2560 * 1280, bytes_accessed=2000000, transcendentals=0
        ),
        name="forward_rows",
    )(waves, grid)


def table_kernel(waves_ref, table_ref):
    waves = waves_ref[...]
    lanes = lax.broadcasted_iota(jnp.int32, waves.shape, 1).astype(F32)
    near_c, near_s = cos_sin(phase_of(waves * lanes))
    far_c, far_s = cos_sin(phase_of(waves * (lanes * 128.0)))
    factor = 1.0 / math.sqrt(NLON)
    far_c = far_c * factor
    far_s = far_s * factor
    for a in range(NLON // 128):
        ca = far_c[:, a : a + 1]
        sa = far_s[:, a : a + 1]
        at = slice(a * 128, (a + 1) * 128)
        table_ref[0, :, at] = (ca * near_c - sa * near_s).astype(BF16)
        table_ref[1, :, at] = (-(sa * near_c) - ca * near_s).astype(BF16)


def inverse_table(waves):
    return pl.pallas_call(
        table_kernel,
        grid=(5,),
        in_specs=[pl.BlockSpec((128, 128), lambda i: (i, 0))],
        out_specs=pl.BlockSpec((2, 128, NLON), lambda i: (0, i, 0)),
        out_shape=jax.ShapeDtypeStruct((2, TOP, NLON), BF16),
        compiler_params=params(LARGE),
        cost_estimate=pl.CostEstimate(
            flops=30000000, bytes_accessed=12000000, transcendentals=0
        ),
        name="inverse_table",
    )(waves)


def basis_kernel(own_ref, leg_ref, straight_ref, turned_ref, rows, joined):
    wave = own_ref[pl.program_id(0)]
    for b in range(TOP // 128):
        at = slice(b * 128, (b + 1) * 128)
        degree = b * 128 + lax.broadcasted_iota(jnp.int32, (BAND, 128), 1)
        rows[b] = jnp.where(degree >= wave, leg_ref[0, :, at].astype(F32), 0.0)
        for li in range(ROWS):
            joined[li * WAVES : (li + 1) * WAVES, at] = rows[
                b, pl.ds(li, WAVES, stride=ROWS), :
            ]
    straight_ref[0] = joined[...].astype(BF16)
    turned_ref[0] = joined[...].T.astype(BF16)


def basis(own, legendre):
    return pl.pallas_call(
        basis_kernel,
        grid=(SLOTS,),
        in_specs=[
            pl.BlockSpec(memory_space=pltpu.SMEM),
            pl.BlockSpec((1, BAND, TOP), lambda i: (i, 0, 0)),
        ],
        out_specs=[
            pl.BlockSpec((1, BAND, TOP), lambda i: (i, 0, 0)),
            pl.BlockSpec((1, TOP, BAND), lambda i: (i, 0, 0)),
        ],
        out_shape=[
            jax.ShapeDtypeStruct((SLOTS, BAND, TOP), BF16),
            jax.ShapeDtypeStruct((SLOTS, TOP, BAND), BF16),
        ],
        scratch_shapes=[
            pltpu.VMEM((TOP // 128, BAND, 128), F32),
            pltpu.VMEM((BAND, TOP), F32),
        ],
        compiler_params=params(),
        cost_estimate=pl.CostEstimate(
            flops=0, bytes_accessed=30000000, transcendentals=0
        ),
        name="basis_rows",
    )(own, legendre)


def partial_kernel(own_ref, turned_ref, got_ref, packed_ref, turned, rows, held, sems):
    pairs = SLOTS // 2
    loads = [
        pltpu.make_async_copy(
            turned_ref.at[pl.ds(2 * pair, 2)], turned.at[pl.ds(2 * pair, 2)], sems.at[pair]
        )
        for pair in range(pairs)
    ]
    for load in reversed(loads):
        load.start()
    rows[...] = got_ref[...].astype(F32)
    held[TOP + pairs * PAIR_ROWS :, :] = jnp.zeros((PACKED - pairs * PAIR_ROWS, K), BF16)

    def product(slot):
        values = jnp.concatenate(
            [
                rows[pl.ds(slot * ROWS + li, WAVES, stride=CHUNK), :]
                for li in range(ROWS)
            ],
            axis=0,
        ).astype(BF16)
        return jnp.dot(turned[slot], values, preferred_element_type=F32).astype(BF16)

    for pair in reversed(range(pairs)):
        unit = own_ref[2 * pair] // UNIT
        base = TOP + pair * PAIR_ROWS
        loads[pair].wait()
        held[base + UNIT : base + UNIT + TOP, :] = product(2 * pair)
        at = pl.multiple_of(base - (UNITS - 1 - unit) * UNIT, UNIT)
        held[pl.ds(at, TOP), :] = product(2 * pair + 1)
    packed_ref[...] = held[TOP:, :]


def partial_sums(own, turned, got):
    return pl.pallas_call(
        partial_kernel,
        in_specs=[
            pl.BlockSpec(memory_space=pltpu.SMEM),
            pl.BlockSpec(memory_space=pl.ANY),
            pl.BlockSpec(memory_space=pltpu.VMEM),
        ],
        out_specs=pl.BlockSpec(memory_space=pltpu.VMEM),
        out_shape=jax.ShapeDtypeStruct((PACKED, K), BF16),
        scratch_shapes=[
            pltpu.VMEM((SLOTS, TOP, BAND), BF16),
            pltpu.VMEM((WAVES * CHUNK, K), F32),
            pltpu.VMEM((TOP + PACKED, K), BF16),
            pltpu.SemaphoreType.DMA((SLOTS // 2,)),
        ],
        compiler_params=pltpu.CompilerParams(vmem_limit_bytes=VMEM_LIMIT),
        cost_estimate=pl.CostEstimate(
            flops=2 * 10 * 192 * 640 * 128, bytes_accessed=5000000, transcendentals=0
        ),
        name="partial_sums",
    )(own, turned, got)


def couple_kernel(own_ref, lat_ref, parts_ref, couple_ref, out_ref):
    total = parts_ref[0].astype(F32)
    for g in range(1, GROUPS):
        total = total + parts_ref[g].astype(F32)
    pulled = jnp.dot(
        total,
        couple_ref[...],
        preferred_element_type=F32,
        precision=lax.Precision.HIGHEST,
    )
    position = lat_ref[0] * SHARE + lax.broadcasted_iota(jnp.int32, (SHARE, K), 0)
    degree = jnp.zeros((SHARE, K), jnp.int32)
    for pair in range(SLOTS // 2):
        unit = own_ref[2 * pair] // UNIT
        inside = position - pair * PAIR_ROWS
        shift = jnp.where(inside >= (unit + 1) * UNIT, -UNIT, (UNITS - 1 - unit) * UNIT)
        degree = jnp.where(inside >= 0, inside + shift, degree)
    degree = degree.astype(F32)
    column = lax.broadcasted_iota(jnp.int32, (SHARE, K), 1)
    factor = jnp.where(
        (column & 63) < 32, degree * (degree + 1.0) / float(TOP * TOP), 1.0
    )
    out_ref[...] = (total - factor * pulled).astype(BF16)


def couple(own, lat, parts, matrix):
    return pl.pallas_call(
        couple_kernel,
        in_specs=[
            pl.BlockSpec(memory_space=pltpu.SMEM),
            pl.BlockSpec(memory_space=pltpu.SMEM),
            pl.BlockSpec(memory_space=pltpu.VMEM),
            pl.BlockSpec(memory_space=pltpu.VMEM),
        ],
        out_specs=pl.BlockSpec(memory_space=pltpu.VMEM),
        out_shape=jax.ShapeDtypeStruct((SHARE, K), BF16),
        compiler_params=pltpu.CompilerParams(vmem_limit_bytes=VMEM_LIMIT),
        cost_estimate=pl.CostEstimate(
            flops=2 * 416 * 128 * 128 * 6, bytes_accessed=1200000, transcendentals=0
        ),
        name="couple_levels",
    )(own, lat, parts, matrix)


def inverse_kernel(
    own_ref, block_ref, straight_ref, all_ref, out_ref, send_ref, straight, held, rows, sems
):
    pairs = SLOTS // 2
    loads = [
        pltpu.make_async_copy(
            straight_ref.at[pl.ds(2 * pair, 2)], straight.at[pl.ds(2 * pair, 2)], sems.at[pair]
        )
        for pair in range(pairs)
    ]
    for load in loads:
        load.start()
    held[:TOP, :] = jnp.zeros((TOP, K), BF16)
    held[TOP:, :] = all_ref[...]
    size = TOP // GROUPS
    begin = block_ref[0] * size
    degree = begin + lax.broadcasted_iota(jnp.int32, (size, K), 0)
    for pair in range(pairs):
        base = TOP + pair * PAIR_ROWS
        unit = own_ref[2 * pair] // UNIT
        loads[pair].wait()
        for q in range(2):
            slot = 2 * pair + q
            wave = own_ref[slot]
            start = base + UNIT if q == 0 else base - (UNITS - 1 - unit) * UNIT
            values = held[pl.ds(pl.multiple_of(start, UNIT), TOP), :]
            back = jnp.dot(straight[slot], values, preferred_element_type=F32)
            back = back * jnp.where(wave == 0, 1.0, 2.0)
            for li in range(ROWS):
                at = slot * ROWS + li
                rows[pl.ds(at, WAVES, stride=CHUNK), :] = back[
                    li * WAVES : (li + 1) * WAVES
                ]
            mine = held[pl.ds(pl.multiple_of(start + begin, UNIT), size), :]
            out_ref[slot] = jnp.where(degree >= wave, mine.astype(F32), 0.0).astype(BF16)
    clear_spare(rows)
    send_ref[...] = rows[...].astype(BF16)


def inverse(own, block, straight, everything):
    return pl.pallas_call(
        inverse_kernel,
        in_specs=[
            pl.BlockSpec(memory_space=pltpu.SMEM),
            pl.BlockSpec(memory_space=pltpu.SMEM),
            pl.BlockSpec(memory_space=pl.ANY),
            pl.BlockSpec(memory_space=pltpu.VMEM),
        ],
        out_specs=[
            pl.BlockSpec(memory_space=pltpu.VMEM),
            pl.BlockSpec(memory_space=pltpu.VMEM),
        ],
        out_shape=[
            jax.ShapeDtypeStruct((SLOTS, TOP // GROUPS, K), BF16),
            jax.ShapeDtypeStruct((WAVES * CHUNK, K), BF16),
        ],
        scratch_shapes=[
            pltpu.VMEM((SLOTS, BAND, TOP), BF16),
            pltpu.VMEM((TOP + PACKED, K), BF16),
            pltpu.VMEM((WAVES * CHUNK, K), F32),
            pltpu.SemaphoreType.DMA((SLOTS // 2,)),
        ],
        compiler_params=pltpu.CompilerParams(vmem_limit_bytes=VMEM_LIMIT),
        cost_estimate=pl.CostEstimate(
            flops=2 * 10 * 192 * 640 * 128, bytes_accessed=5000000, transcendentals=0
        ),
        name="inverse_sums",
    )(own, block, straight, everything)


def finish_kernel(got_ref, table_ref, out_ref, table, made, rows, left, loads, stores):
    parts, _, _, block = table.shape

    def load(part):
        at = pl.ds(part * block, block)
        return pltpu.make_async_copy(
            table_ref.at[:, :, at], table.at[part], loads.at[part]
        )

    def store(part):
        at = pl.ds(part * block, block)
        return pltpu.make_async_copy(made.at[part], out_ref.at[:, at], stores.at[part])

    for part in range(parts):
        load(part).start()
    rows[...] = got_ref[...].astype(F32)
    for li in range(ROWS):
        values = jnp.concatenate(
            [
                rows[pl.ds(slot * ROWS + li, WAVES, stride=CHUNK), :]
                for slot in range(SLOTS)
            ],
            axis=0,
        )
        turned = values.T.astype(BF16)
        at = slice(li * FIELDS, (li + 1) * FIELDS)
        left[at, :TOP] = turned[:FIELDS]
        left[at, TOP:] = turned[FIELDS:]
    for part in range(parts):
        load(part).wait()
        right = table[part].reshape(2 * TOP, block)
        made[part] = jnp.dot(left[...], right, preferred_element_type=F32).astype(BF16)
        store(part).start()
    for part in range(parts):
        store(part).wait()


def finish(got, table):
    parts = 5
    block = NLON // parts
    return pl.pallas_call(
        finish_kernel,
        in_specs=[
            pl.BlockSpec(memory_space=pltpu.VMEM),
            pl.BlockSpec(memory_space=pl.ANY),
        ],
        out_specs=pl.BlockSpec(memory_space=pl.ANY),
        out_shape=jax.ShapeDtypeStruct((ROWS * FIELDS, NLON), BF16),
        scratch_shapes=[
            pltpu.VMEM((parts, 2, TOP, block), BF16),
            pltpu.VMEM((parts, ROWS * FIELDS, block), BF16),
            pltpu.VMEM((WAVES * CHUNK, K), F32),
            pltpu.VMEM((ROWS * FIELDS, 2 * TOP), BF16),
            pltpu.SemaphoreType.DMA((parts,)),
            pltpu.SemaphoreType.DMA((parts,)),
        ],
        compiler_params=pltpu.CompilerParams(vmem_limit_bytes=MIDDLE),
        cost_estimate=pl.CostEstimate(
            flops=2 * 192 * 2560 * 1280, bytes_accessed=9000000, transcendentals=0
        ),
        name="finish_rows",
    )(got, table)


def coupling_matrix(couple_div, couple_temp):
    zero = jnp.zeros_like(couple_div)
    one = jnp.block([[zero, couple_temp.T], [couple_div.T, zero]])
    none = jnp.zeros_like(one)
    return jnp.block([[one, none], [none, one]])


def body(grid_in, legendre, wave_order, block_order, couple_div, couple_temp):
    lat = lax.axis_index("lat")
    wave = lax.axis_index("wave")
    send = forward(wave_order, grid_in.reshape(ROWS * FIELDS, NLON))
    swap = functools.partial(lax.all_to_all, split_axis=0, concat_axis=0, tiled=True)
    got = swap(send.reshape(WAVES, CHUNK, K), "wave")
    own = lax.dynamic_slice_in_dim(wave_order, wave * SLOTS, SLOTS)
    block = lax.dynamic_slice_in_dim(block_order, lat, 1)
    straight, turned = basis(own, legendre)
    waves = wave_order.reshape(WAVES, SLOTS).T.reshape(TOP, 1).astype(F32)
    table = inverse_table(jnp.broadcast_to(waves, (TOP, 128)))
    matrix = coupling_matrix(couple_div, couple_temp)
    packed = partial_sums(own, turned, got.reshape(WAVES * CHUNK, K))
    parts = swap(packed.reshape(GROUPS, SHARE, K), "lat")
    spectral = couple(own, lat.reshape(1), parts, matrix)
    everything = lax.all_gather(spectral, "lat", axis=0, tiled=True)
    spectral_out, send = inverse(own, block, straight, everything)
    got = swap(send.reshape(WAVES, CHUNK, K), "wave")
    grid_out = finish(got.reshape(WAVES * CHUNK, K), table)
    return spectral_out.transpose(1, 0, 2), grid_out.reshape(ROWS, FIELDS, NLON)


def solution(mesh):
    placed = (P(("lat", "wave"), None, None), P("wave", "lat", None), P(), P(), P(), P())
    return jax.shard_map(
        body,
        mesh=mesh,
        in_specs=placed,
        out_specs=(P("lat", "wave", None), P(("lat", "wave"), None, None)),
        check_vma=False,
    )
```

```python
import functools
import math

import jax
import jax.numpy as jnp
from jax import lax
from jax.experimental import pallas as pl
from jax.experimental.pallas import tpu as pltpu
from jax.sharding import PartitionSpec as P

F32 = jnp.float32
BF16 = jnp.bfloat16
NLON = 2560
WAVES = 64
GROUPS = 8
SLOTS = 10
ROWS = 3
FIELDS = 64
K = 128
TOP = 640
BAND = 192
CHUNK = 32
LINE = CHUNK + 1
UNIT = 16
UNITS = TOP // UNIT
PAIR_ROWS = TOP + UNIT
PACKED = 3328
SHARE = PACKED // GROUPS
VMEM_LIMIT = 24 * 1024 * 1024
LARGE = 58 * 1024 * 1024
MIDDLE = 50 * 1024 * 1024


def params(limit=VMEM_LIMIT):
    return pltpu.CompilerParams(
        dimension_semantics=("arbitrary",), vmem_limit_bytes=limit
    )


def cos_sin(phase):
    quarter = (
        (phase >= 320.0).astype(F32)
        + (phase >= 960.0).astype(F32)
        + (phase >= 1600.0).astype(F32)
        + (phase >= 2240.0).astype(F32)
    )
    x = (phase - 640.0 * quarter) * (2.0 * math.pi / NLON)
    y = x * x
    s = x * (
        1.0 + y * (-1.0 / 6 + y * (1.0 / 120 + y * (-1.0 / 5040 + y * (1.0 / 362880))))
    )
    c = 1.0 + y * (
        -0.5 + y * (1.0 / 24 + y * (-1.0 / 720 + y * (1.0 / 40320 + y * (-1.0 / 3628800))))
    )
    odd = (quarter == 1.0) | (quarter == 3.0)
    cos = jnp.where(odd, s, c)
    sin = jnp.where(odd, c, s)
    cos = jnp.where((quarter == 1.0) | (quarter == 2.0), -cos, cos)
    sin = jnp.where((quarter == 2.0) | (quarter == 3.0), -sin, sin)
    return cos, sin


def phase_of(product):
    return product - NLON * jnp.floor((product + 0.5) * (1.0 / NLON))


def forward_kernel(waves_ref, grid_ref, send_ref, grid, lines, rows, sem):
    step = pl.program_id(0)
    load = pltpu.make_async_copy(grid_ref, grid, sem)

    @pl.when(step == 0)
    def _():
        load.start()

    waves = jnp.zeros((1, 128), F32)
    for part in range(TOP // 128):
        one = waves_ref[part * 128 : (part + 1) * 128].astype(F32).reshape(1, 128)
        waves = jnp.where(step == part, one, waves)
    down = lax.broadcasted_iota(jnp.int32, (128, 128), 0).astype(F32)
    near_c, near_s = cos_sin(phase_of(waves * down))
    far_c, far_s = cos_sin(phase_of(waves * (down[:16] * 128.0)))
    factor = 1.0 / math.sqrt(NLON)
    far_c = far_c * factor
    far_s = far_s * factor
    sign = 1.0 - 2.0 * (waves - 2.0 * jnp.floor(waves * 0.5))

    @pl.when(step == 0)
    def _():
        load.wait()

    made = jnp.zeros((ROWS * FIELDS, 256), F32)
    half = NLON // 2
    for a in range(half // 128):
        ca = far_c[a : a + 1]
        sa = far_s[a : a + 1]
        c = ca * near_c - sa * near_s
        s = -(sa * near_c) - ca * near_s
        first = jnp.concatenate([c, s], axis=1).astype(BF16)
        second = jnp.concatenate([c * sign, s * sign], axis=1).astype(BF16)
        left = jnp.concatenate(
            [
                grid[:, a * 128 : (a + 1) * 128],
                grid[:, half + a * 128 : half + (a + 1) * 128],
            ],
            axis=1,
        )
        right = jnp.concatenate([first, second], axis=0)
        made = made + jnp.dot(left, right, preferred_element_type=F32)
    at = pl.ds(pl.multiple_of(step * 128, 128), 128)
    for li in range(ROWS):
        one = made[li * FIELDS : (li + 1) * FIELDS]
        lines[li, at, :] = jnp.concatenate([one[:, :128], one[:, 128:]], axis=0).T

    @pl.when(step == TOP // 128 - 1)
    def _():
        for li in range(ROWS):
            for slot in range(SLOTS):
                rows[pl.ds(slot * ROWS + li, WAVES, stride=LINE), :] = lines[
                    li, pl.ds(slot, WAVES, stride=SLOTS), :
                ]
        clear_spare(rows)
        tighten(rows, send_ref)


def clear_spare(rows):
    for row in range(SLOTS * ROWS, CHUNK):
        rows[pl.ds(row, WAVES, stride=LINE), :] = jnp.zeros((WAVES, K), F32)


def tighten(rows, out):
    for wave in range(WAVES):
        out[wave * CHUNK : (wave + 1) * CHUNK, :] = rows[
            wave * LINE : wave * LINE + CHUNK, :
        ].astype(BF16)


def loosen(got, rows):
    for wave in range(WAVES):
        rows[wave * LINE : wave * LINE + CHUNK, :] = got[
            wave * CHUNK : (wave + 1) * CHUNK, :
        ].astype(F32)


def forward(waves, grid):
    return pl.pallas_call(
        forward_kernel,
        grid=(TOP // 128,),
        in_specs=[
            pl.BlockSpec((TOP,), lambda i: (0,)),
            pl.BlockSpec(memory_space=pl.ANY),
        ],
        out_specs=pl.BlockSpec((WAVES * CHUNK, K), lambda i: (0, 0)),
        out_shape=jax.ShapeDtypeStruct((WAVES * CHUNK, K), BF16),
        scratch_shapes=[
            pltpu.VMEM((ROWS * FIELDS, NLON), BF16),
            pltpu.VMEM((ROWS, TOP, K), F32),
            pltpu.VMEM((WAVES * LINE, K), F32),
            pltpu.SemaphoreType.DMA,
        ],
        compiler_params=params(LARGE),
        cost_estimate=pl.CostEstimate(
            flops=2 * 192 * 2560 * 1280, bytes_accessed=2000000, transcendentals=0
        ),
        name="forward_rows",
    )(waves, grid)


def table_kernel(waves_ref, table_ref):
    waves = waves_ref[...]
    lanes = lax.broadcasted_iota(jnp.int32, waves.shape, 1).astype(F32)
    near_c, near_s = cos_sin(phase_of(waves * lanes))
    far_c, far_s = cos_sin(phase_of(waves * (lanes * 128.0)))
    factor = 1.0 / math.sqrt(NLON)
    far_c = far_c * factor
    far_s = far_s * factor
    for a in range(NLON // 128):
        ca = far_c[:, a : a + 1]
        sa = far_s[:, a : a + 1]
        at = slice(a * 128, (a + 1) * 128)
        table_ref[0, :, at] = (ca * near_c - sa * near_s).astype(BF16)
        table_ref[1, :, at] = (-(sa * near_c) - ca * near_s).astype(BF16)


def inverse_table(waves):
    return pl.pallas_call(
        table_kernel,
        grid=(5,),
        in_specs=[pl.BlockSpec((128, 128), lambda i: (i, 0))],
        out_specs=pl.BlockSpec((2, 128, NLON), lambda i: (0, i, 0)),
        out_shape=jax.ShapeDtypeStruct((2, TOP, NLON), BF16),
        compiler_params=params(LARGE),
        cost_estimate=pl.CostEstimate(
            flops=30000000, bytes_accessed=12000000, transcendentals=0
        ),
        name="inverse_table",
    )(waves)


def basis_kernel(own_ref, leg_ref, straight_ref, turned_ref, rows, joined):
    wave = own_ref[pl.program_id(0)]
    for b in range(TOP // 128):
        at = slice(b * 128, (b + 1) * 128)
        degree = b * 128 + lax.broadcasted_iota(jnp.int32, (BAND, 128), 1)
        rows[b] = jnp.where(degree >= wave, leg_ref[0, :, at].astype(F32), 0.0)
        for li in range(ROWS):
            joined[li * WAVES : (li + 1) * WAVES, at] = rows[
                b, pl.ds(li, WAVES, stride=ROWS), :
            ]
    straight_ref[0] = joined[...].astype(BF16)
    turned_ref[0] = joined[...].T.astype(BF16)


def basis(own, legendre):
    return pl.pallas_call(
        basis_kernel,
        grid=(SLOTS,),
        in_specs=[
            pl.BlockSpec(memory_space=pltpu.SMEM),
            pl.BlockSpec((1, BAND, TOP), lambda i: (i, 0, 0)),
        ],
        out_specs=[
            pl.BlockSpec((1, BAND, TOP), lambda i: (i, 0, 0)),
            pl.BlockSpec((1, TOP, BAND), lambda i: (i, 0, 0)),
        ],
        out_shape=[
            jax.ShapeDtypeStruct((SLOTS, BAND, TOP), BF16),
            jax.ShapeDtypeStruct((SLOTS, TOP, BAND), BF16),
        ],
        scratch_shapes=[
            pltpu.VMEM((TOP // 128, BAND, 128), F32),
            pltpu.VMEM((BAND, TOP), F32),
        ],
        compiler_params=params(),
        cost_estimate=pl.CostEstimate(
            flops=0, bytes_accessed=30000000, transcendentals=0
        ),
        name="basis_rows",
    )(own, legendre)


def partial_kernel(own_ref, turned_ref, got_ref, packed_ref, rows, held):
    step = pl.program_id(0)
    pair = 4 - step

    @pl.when(step == 0)
    def _():
        loosen(got_ref, rows)
        held[TOP + 5 * PAIR_ROWS :, :] = jnp.zeros((PACKED - 5 * PAIR_ROWS, K), BF16)

    def product(q):
        slot = 2 * pair + q
        values = jnp.concatenate(
            [
                rows[pl.ds(slot * ROWS + li, WAVES, stride=LINE), :]
                for li in range(ROWS)
            ],
            axis=0,
        ).astype(BF16)
        return jnp.dot(turned_ref[q], values, preferred_element_type=F32).astype(BF16)

    unit = own_ref[2 * pair] // UNIT
    base = TOP + pair * PAIR_ROWS
    held[pl.ds(pl.multiple_of(base + UNIT, UNIT), TOP), :] = product(0)
    at = pl.multiple_of(base - (UNITS - 1 - unit) * UNIT, UNIT)
    held[pl.ds(at, TOP), :] = product(1)

    @pl.when(step == 4)
    def _():
        packed_ref[...] = held[TOP:, :]


def partial_sums(own, turned, got):
    return pl.pallas_call(
        partial_kernel,
        grid=(5,),
        in_specs=[
            pl.BlockSpec(memory_space=pltpu.SMEM),
            pl.BlockSpec((2, TOP, BAND), lambda i: (4 - i, 0, 0)),
            pl.BlockSpec((WAVES * CHUNK, K), lambda i: (0, 0)),
        ],
        out_specs=pl.BlockSpec((PACKED, K), lambda i: (0, 0)),
        out_shape=jax.ShapeDtypeStruct((PACKED, K), BF16),
        scratch_shapes=[
            pltpu.VMEM((WAVES * LINE, K), F32),
            pltpu.VMEM((TOP + PACKED, K), BF16),
        ],
        compiler_params=params(),
        cost_estimate=pl.CostEstimate(
            flops=2 * 10 * 192 * 640 * 128, bytes_accessed=5000000, transcendentals=0
        ),
        name="partial_sums",
    )(own, turned, got)


def couple_kernel(own_ref, lat_ref, parts_ref, couple_ref, out_ref):
    total = parts_ref[0].astype(F32)
    for g in range(1, GROUPS):
        total = total + parts_ref[g].astype(F32)
    pulled = jnp.dot(
        total,
        couple_ref[...],
        preferred_element_type=F32,
        precision=lax.Precision.HIGHEST,
    )
    position = lat_ref[0] * SHARE + lax.broadcasted_iota(jnp.int32, (SHARE, K), 0)
    degree = jnp.zeros((SHARE, K), jnp.int32)
    for pair in range(SLOTS // 2):
        unit = own_ref[2 * pair] // UNIT
        inside = position - pair * PAIR_ROWS
        shift = jnp.where(inside >= (unit + 1) * UNIT, -UNIT, (UNITS - 1 - unit) * UNIT)
        degree = jnp.where(inside >= 0, inside + shift, degree)
    degree = degree.astype(F32)
    column = lax.broadcasted_iota(jnp.int32, (SHARE, K), 1)
    factor = jnp.where(
        (column & 63) < 32, degree * (degree + 1.0) / float(TOP * TOP), 1.0
    )
    out_ref[...] = (total - factor * pulled).astype(BF16)


def couple(own, lat, parts, matrix):
    return pl.pallas_call(
        couple_kernel,
        in_specs=[
            pl.BlockSpec(memory_space=pltpu.SMEM),
            pl.BlockSpec(memory_space=pltpu.SMEM),
            pl.BlockSpec(memory_space=pltpu.VMEM),
            pl.BlockSpec(memory_space=pltpu.VMEM),
        ],
        out_specs=pl.BlockSpec(memory_space=pltpu.VMEM),
        out_shape=jax.ShapeDtypeStruct((SHARE, K), BF16),
        compiler_params=pltpu.CompilerParams(vmem_limit_bytes=VMEM_LIMIT),
        cost_estimate=pl.CostEstimate(
            flops=2 * 416 * 128 * 128 * 6, bytes_accessed=1200000, transcendentals=0
        ),
        name="couple_levels",
    )(own, lat, parts, matrix)


def inverse_kernel(own_ref, block_ref, straight_ref, all_ref, out_ref, send_ref, held, rows):
    step = pl.program_id(0)

    @pl.when(step == 0)
    def _():
        held[:TOP, :] = jnp.zeros((TOP, K), BF16)
        held[TOP:, :] = all_ref[...]

    base = TOP + step * PAIR_ROWS
    unit = own_ref[2 * step] // UNIT
    size = TOP // GROUPS
    begin = block_ref[0] * size
    degree = begin + lax.broadcasted_iota(jnp.int32, (size, K), 0)
    for q in range(2):
        wave = own_ref[2 * step + q]
        start = base + UNIT if q == 0 else base - (UNITS - 1 - unit) * UNIT
        values = held[pl.ds(pl.multiple_of(start, UNIT), TOP), :]
        back = jnp.dot(straight_ref[q], values, preferred_element_type=F32)
        back = back * jnp.where(wave == 0, 1.0, 2.0)
        for li in range(ROWS):
            at = (2 * step + q) * ROWS + li
            rows[pl.ds(at, WAVES, stride=LINE), :] = back[li * WAVES : (li + 1) * WAVES]
        mine = held[pl.ds(pl.multiple_of(start + begin, UNIT), size), :]
        out_ref[q] = jnp.where(degree >= wave, mine.astype(F32), 0.0).astype(BF16)

    @pl.when(step == 4)
    def _():
        clear_spare(rows)
        tighten(rows, send_ref)


def inverse(own, block, straight, everything):
    return pl.pallas_call(
        inverse_kernel,
        grid=(5,),
        in_specs=[
            pl.BlockSpec(memory_space=pltpu.SMEM),
            pl.BlockSpec(memory_space=pltpu.SMEM),
            pl.BlockSpec((2, BAND, TOP), lambda i: (i, 0, 0)),
            pl.BlockSpec((PACKED, K), lambda i: (0, 0)),
        ],
        out_specs=[
            pl.BlockSpec((2, TOP // GROUPS, K), lambda i: (i, 0, 0)),
            pl.BlockSpec((WAVES * CHUNK, K), lambda i: (0, 0)),
        ],
        out_shape=[
            jax.ShapeDtypeStruct((SLOTS, TOP // GROUPS, K), BF16),
            jax.ShapeDtypeStruct((WAVES * CHUNK, K), BF16),
        ],
        scratch_shapes=[
            pltpu.VMEM((TOP + PACKED, K), BF16),
            pltpu.VMEM((WAVES * LINE, K), F32),
        ],
        compiler_params=params(),
        cost_estimate=pl.CostEstimate(
            flops=2 * 10 * 192 * 640 * 128, bytes_accessed=5000000, transcendentals=0
        ),
        name="inverse_sums",
    )(own, block, straight, everything)


def finish_kernel(got_ref, table_ref, out_ref, table, made, rows, left, loads, stores):
    parts, _, _, block = table.shape

    def load(part):
        at = pl.ds(part * block, block)
        return pltpu.make_async_copy(
            table_ref.at[:, :, at], table.at[part], loads.at[part]
        )

    def store(part):
        at = pl.ds(part * block, block)
        return pltpu.make_async_copy(made.at[part], out_ref.at[:, at], stores.at[part])

    for part in range(parts):
        load(part).start()
    loosen(got_ref, rows)
    for li in range(ROWS):
        values = jnp.concatenate(
            [
                rows[pl.ds(slot * ROWS + li, WAVES, stride=LINE), :]
                for slot in range(SLOTS)
            ],
            axis=0,
        )
        turned = values.T.astype(BF16)
        at = slice(li * FIELDS, (li + 1) * FIELDS)
        left[at, :TOP] = turned[:FIELDS]
        left[at, TOP:] = turned[FIELDS:]
    for part in range(parts):
        load(part).wait()
        right = table[part].reshape(2 * TOP, block)
        made[part] = jnp.dot(left[...], right, preferred_element_type=F32).astype(BF16)
        store(part).start()
    for part in range(parts):
        store(part).wait()


def finish(got, table):
    parts = 5
    block = NLON // parts
    return pl.pallas_call(
        finish_kernel,
        in_specs=[
            pl.BlockSpec(memory_space=pltpu.VMEM),
            pl.BlockSpec(memory_space=pl.ANY),
        ],
        out_specs=pl.BlockSpec(memory_space=pl.ANY),
        out_shape=jax.ShapeDtypeStruct((ROWS * FIELDS, NLON), BF16),
        scratch_shapes=[
            pltpu.VMEM((parts, 2, TOP, block), BF16),
            pltpu.VMEM((parts, ROWS * FIELDS, block), BF16),
            pltpu.VMEM((WAVES * LINE, K), F32),
            pltpu.VMEM((ROWS * FIELDS, 2 * TOP), BF16),
            pltpu.SemaphoreType.DMA((parts,)),
            pltpu.SemaphoreType.DMA((parts,)),
        ],
        compiler_params=pltpu.CompilerParams(vmem_limit_bytes=MIDDLE),
        cost_estimate=pl.CostEstimate(
            flops=2 * 192 * 2560 * 1280, bytes_accessed=9000000, transcendentals=0
        ),
        name="finish_rows",
    )(got, table)


def coupling_matrix(couple_div, couple_temp):
    zero = jnp.zeros_like(couple_div)
    one = jnp.block([[zero, couple_temp.T], [couple_div.T, zero]])
    none = jnp.zeros_like(one)
    return jnp.block([[one, none], [none, one]])


def body(grid_in, legendre, wave_order, block_order, couple_div, couple_temp):
    lat = lax.axis_index("lat")
    wave = lax.axis_index("wave")
    send = forward(wave_order, grid_in.reshape(ROWS * FIELDS, NLON))
    swap = functools.partial(lax.all_to_all, split_axis=0, concat_axis=0, tiled=True)
    got = swap(send.reshape(WAVES, CHUNK, K), "wave")
    own = lax.dynamic_slice_in_dim(wave_order, wave * SLOTS, SLOTS)
    block = lax.dynamic_slice_in_dim(block_order, lat, 1)
    straight, turned = basis(own, legendre)
    waves = wave_order.reshape(WAVES, SLOTS).T.reshape(TOP, 1).astype(F32)
    table = inverse_table(jnp.broadcast_to(waves, (TOP, 128)))
    matrix = coupling_matrix(couple_div, couple_temp)
    packed = partial_sums(own, turned, got.reshape(WAVES * CHUNK, K))
    parts = swap(packed.reshape(GROUPS, SHARE, K), "lat")
    spectral = couple(own, lat.reshape(1), parts, matrix)
    everything = lax.all_gather(spectral, "lat", axis=0, tiled=True)
    spectral_out, send = inverse(own, block, straight, everything)
    got = swap(send.reshape(WAVES, CHUNK, K), "wave")
    grid_out = finish(got.reshape(WAVES * CHUNK, K), table)
    return spectral_out.transpose(1, 0, 2), grid_out.reshape(ROWS, FIELDS, NLON)


def solution(mesh):
    placed = (P(("lat", "wave"), None, None), P("wave", "lat", None), P(), P(), P(), P())
    return jax.shard_map(
        body,
        mesh=mesh,
        in_specs=placed,
        out_specs=(P("lat", "wave", None), P(("lat", "wave"), None, None)),
        check_vma=False,
    )
```

```python
import functools
import math

import jax
import jax.numpy as jnp
from jax import lax
from jax.experimental import pallas as pl
from jax.experimental.pallas import tpu as pltpu
from jax.sharding import PartitionSpec as P

F32 = jnp.float32
BF16 = jnp.bfloat16
NLON = 2560
HALF = NLON // 2
WAVES = 64
GROUPS = 8
SLOTS = 10
ROWS = 3
FIELDS = 64
K = 128
TOP = 640
BAND = 192
CHUNK = 32
LINE = CHUNK + 1
UNIT = 16
UNITS = TOP // UNIT
PAIR_ROWS = TOP + UNIT
PACKED = 3328
SHARE = PACKED // GROUPS
VMEM_LIMIT = 24 * 1024 * 1024
LARGE = 58 * 1024 * 1024
MIDDLE = 52 * 1024 * 1024


def params(limit=VMEM_LIMIT):
    return pltpu.CompilerParams(
        dimension_semantics=("arbitrary",), vmem_limit_bytes=limit
    )


def cos_sin(phase):
    quarter = (
        (phase >= 320.0).astype(F32)
        + (phase >= 960.0).astype(F32)
        + (phase >= 1600.0).astype(F32)
        + (phase >= 2240.0).astype(F32)
    )
    x = (phase - 640.0 * quarter) * (2.0 * math.pi / NLON)
    y = x * x
    s = x * (
        1.0 + y * (-1.0 / 6 + y * (1.0 / 120 + y * (-1.0 / 5040 + y * (1.0 / 362880))))
    )
    c = 1.0 + y * (
        -0.5 + y * (1.0 / 24 + y * (-1.0 / 720 + y * (1.0 / 40320 + y * (-1.0 / 3628800))))
    )
    odd = (quarter == 1.0) | (quarter == 3.0)
    cos = jnp.where(odd, s, c)
    sin = jnp.where(odd, c, s)
    cos = jnp.where((quarter == 1.0) | (quarter == 2.0), -cos, cos)
    sin = jnp.where((quarter == 2.0) | (quarter == 3.0), -sin, sin)
    return cos, sin


def phase_of(product):
    return product - NLON * jnp.floor((product + 0.5) * (1.0 / NLON))


def forward_kernel(waves_ref, grid_ref, send_ref, grid, near, far, lines, rows, sem):
    step = pl.program_id(0)

    @pl.when(step == 0)
    def _():
        load = pltpu.make_async_copy(grid_ref, grid, sem)
        load.start()
        waves = waves_ref[...].astype(F32).reshape(1, TOP)
        down = lax.broadcasted_iota(jnp.int32, (128, TOP), 0).astype(F32)
        c, s = cos_sin(phase_of(waves * down))
        near[0] = c
        near[1] = s
        c, s = cos_sin(phase_of(waves * (down[:16] * 128.0)))
        factor = 1.0 / math.sqrt(NLON)
        far[0] = c * factor
        far[1] = s * factor
        load.wait()

    at = pl.ds(pl.multiple_of(step * 128, 128), 128)
    near_c = near[0, :, at]
    near_s = near[1, :, at]
    far_c = far[0, :, at]
    far_s = far[1, :, at]
    made = jnp.zeros((2 * ROWS * FIELDS, 256), F32)
    for a in range(0, HALF // 128, 2):
        right = []
        for b in (a, a + 1):
            ca = far_c[b : b + 1]
            sa = far_s[b : b + 1]
            c = ca * near_c - sa * near_s
            s = -(sa * near_c) - ca * near_s
            right.append(jnp.concatenate([c, s], axis=1).astype(BF16))
        left = jnp.concatenate(
            [
                grid[:, a * 128 : (a + 2) * 128],
                grid[:, HALF + a * 128 : HALF + (a + 2) * 128],
            ],
            axis=0,
        )
        made = made + jnp.dot(
            left, jnp.concatenate(right, axis=0), preferred_element_type=F32
        )
    sign = jnp.where(far_c[HALF // 128 : HALF // 128 + 1] > 0.0, 1.0, -1.0)
    sign = jnp.concatenate([sign, sign], axis=1)
    made = made[: ROWS * FIELDS] + sign * made[ROWS * FIELDS :]
    for li in range(ROWS):
        one = made[li * FIELDS : (li + 1) * FIELDS]
        lines[li, at, :] = jnp.concatenate([one[:, :128], one[:, 128:]], axis=0).T

    @pl.when(step == TOP // 128 - 1)
    def _():
        for li in range(ROWS):
            for slot in range(SLOTS):
                rows[pl.ds(slot * ROWS + li, WAVES, stride=LINE), :] = lines[
                    li, pl.ds(slot, WAVES, stride=SLOTS), :
                ]
        clear_spare(rows)
        tighten(rows, send_ref)


def clear_spare(rows):
    for row in range(SLOTS * ROWS, CHUNK):
        rows[pl.ds(row, WAVES, stride=LINE), :] = jnp.zeros((WAVES, K), F32)


def tighten(rows, out):
    for wave in range(WAVES):
        out[wave * CHUNK : (wave + 1) * CHUNK, :] = rows[
            wave * LINE : wave * LINE + CHUNK, :
        ].astype(BF16)


def loosen(got, rows):
    for wave in range(WAVES):
        rows[wave * LINE : wave * LINE + CHUNK, :] = got[
            wave * CHUNK : (wave + 1) * CHUNK, :
        ].astype(F32)


def forward(waves, grid):
    return pl.pallas_call(
        forward_kernel,
        grid=(TOP // 128,),
        in_specs=[
            pl.BlockSpec((TOP,), lambda i: (0,)),
            pl.BlockSpec(memory_space=pl.ANY),
        ],
        out_specs=pl.BlockSpec((WAVES * CHUNK, K), lambda i: (0, 0)),
        out_shape=jax.ShapeDtypeStruct((WAVES * CHUNK, K), BF16),
        scratch_shapes=[
            pltpu.VMEM((ROWS * FIELDS, NLON), BF16),
            pltpu.VMEM((2, 128, TOP), F32),
            pltpu.VMEM((2, 16, TOP), F32),
            pltpu.VMEM((ROWS, TOP, K), F32),
            pltpu.VMEM((WAVES * LINE, K), F32),
            pltpu.SemaphoreType.DMA,
        ],
        compiler_params=params(LARGE),
        cost_estimate=pl.CostEstimate(
            flops=2 * 192 * 2560 * 1280, bytes_accessed=2000000, transcendentals=0
        ),
        name="forward_rows",
    )(waves, grid)


def table_kernel(waves_ref, table_ref):
    waves = waves_ref[...]
    lanes = lax.broadcasted_iota(jnp.int32, waves.shape, 1).astype(F32)
    near_c, near_s = cos_sin(phase_of(waves * lanes))
    far_c, far_s = cos_sin(phase_of(waves * (lanes * 128.0)))
    factor = 1.0 / math.sqrt(NLON)
    far_c = far_c * factor
    far_s = far_s * factor
    for a in range(HALF // 128):
        ca = far_c[:, a : a + 1]
        sa = far_s[:, a : a + 1]
        at = slice(a * 128, (a + 1) * 128)
        table_ref[0, :, at] = (ca * near_c - sa * near_s).astype(BF16)
        table_ref[1, :, at] = (-(sa * near_c) - ca * near_s).astype(BF16)


def inverse_table(waves):
    return pl.pallas_call(
        table_kernel,
        grid=(5,),
        in_specs=[pl.BlockSpec((128, 128), lambda i: (i, 0))],
        out_specs=pl.BlockSpec((2, 128, HALF), lambda i: (0, i, 0)),
        out_shape=jax.ShapeDtypeStruct((2, TOP, HALF), BF16),
        compiler_params=params(LARGE),
        cost_estimate=pl.CostEstimate(
            flops=30000000, bytes_accessed=6000000, transcendentals=0
        ),
        name="inverse_table",
    )(waves)


def basis_kernel(own_ref, leg_ref, straight_ref, turned_ref, rows, joined):
    wave = own_ref[pl.program_id(0)]
    for b in range(TOP // 128):
        at = slice(b * 128, (b + 1) * 128)
        degree = b * 128 + lax.broadcasted_iota(jnp.int32, (BAND, 128), 1)
        rows[b] = jnp.where(degree >= wave, leg_ref[0, :, at].astype(F32), 0.0)
        for li in range(ROWS):
            joined[li * WAVES : (li + 1) * WAVES, at] = rows[
                b, pl.ds(li, WAVES, stride=ROWS), :
            ]
    straight_ref[0] = joined[...].astype(BF16)
    turned_ref[0] = joined[...].T.astype(BF16)


def basis(own, legendre):
    return pl.pallas_call(
        basis_kernel,
        grid=(SLOTS,),
        in_specs=[
            pl.BlockSpec(memory_space=pltpu.SMEM),
            pl.BlockSpec((1, BAND, TOP), lambda i: (i, 0, 0)),
        ],
        out_specs=[
            pl.BlockSpec((1, BAND, TOP), lambda i: (i, 0, 0)),
            pl.BlockSpec((1, TOP, BAND), lambda i: (i, 0, 0)),
        ],
        out_shape=[
            jax.ShapeDtypeStruct((SLOTS, BAND, TOP), BF16),
            jax.ShapeDtypeStruct((SLOTS, TOP, BAND), BF16),
        ],
        scratch_shapes=[
            pltpu.VMEM((TOP // 128, BAND, 128), F32),
            pltpu.VMEM((BAND, TOP), F32),
        ],
        compiler_params=params(),
        cost_estimate=pl.CostEstimate(
            flops=0, bytes_accessed=30000000, transcendentals=0
        ),
        name="basis_rows",
    )(own, legendre)


def partial_kernel(own_ref, turned_ref, got_ref, packed_ref, rows, held):
    step = pl.program_id(0)
    pair = 4 - step

    @pl.when(step == 0)
    def _():
        loosen(got_ref, rows)
        held[TOP + 5 * PAIR_ROWS :, :] = jnp.zeros((PACKED - 5 * PAIR_ROWS, K), BF16)

    def product(q):
        slot = 2 * pair + q
        values = jnp.concatenate(
            [
                rows[pl.ds(slot * ROWS + li, WAVES, stride=LINE), :]
                for li in range(ROWS)
            ],
            axis=0,
        ).astype(BF16)
        return jnp.dot(turned_ref[q], values, preferred_element_type=F32).astype(BF16)

    unit = own_ref[2 * pair] // UNIT
    base = TOP + pair * PAIR_ROWS
    held[pl.ds(pl.multiple_of(base + UNIT, UNIT), TOP), :] = product(0)
    at = pl.multiple_of(base - (UNITS - 1 - unit) * UNIT, UNIT)
    held[pl.ds(at, TOP), :] = product(1)

    @pl.when(step == 4)
    def _():
        packed_ref[...] = held[TOP:, :]


def partial_sums(own, turned, got):
    return pl.pallas_call(
        partial_kernel,
        grid=(5,),
        in_specs=[
            pl.BlockSpec(memory_space=pltpu.SMEM),
            pl.BlockSpec((2, TOP, BAND), lambda i: (4 - i, 0, 0)),
            pl.BlockSpec((WAVES * CHUNK, K), lambda i: (0, 0)),
        ],
        out_specs=pl.BlockSpec((PACKED, K), lambda i: (0, 0)),
        out_shape=jax.ShapeDtypeStruct((PACKED, K), BF16),
        scratch_shapes=[
            pltpu.VMEM((WAVES * LINE, K), F32),
            pltpu.VMEM((TOP + PACKED, K), BF16),
        ],
        compiler_params=params(),
        cost_estimate=pl.CostEstimate(
            flops=2 * 10 * 192 * 640 * 128, bytes_accessed=5000000, transcendentals=0
        ),
        name="partial_sums",
    )(own, turned, got)


def couple_kernel(own_ref, lat_ref, parts_ref, couple_ref, out_ref):
    total = parts_ref[0].astype(F32)
    for g in range(1, GROUPS):
        total = total + parts_ref[g].astype(F32)
    pulled = jnp.dot(
        total,
        couple_ref[...],
        preferred_element_type=F32,
        precision=lax.Precision.HIGHEST,
    )
    position = lat_ref[0] * SHARE + lax.broadcasted_iota(jnp.int32, (SHARE, K), 0)
    degree = jnp.zeros((SHARE, K), jnp.int32)
    for pair in range(SLOTS // 2):
        unit = own_ref[2 * pair] // UNIT
        inside = position - pair * PAIR_ROWS
        shift = jnp.where(inside >= (unit + 1) * UNIT, -UNIT, (UNITS - 1 - unit) * UNIT)
        degree = jnp.where(inside >= 0, inside + shift, degree)
    degree = degree.astype(F32)
    column = lax.broadcasted_iota(jnp.int32, (SHARE, K), 1)
    factor = jnp.where(
        (column & 63) < 32, degree * (degree + 1.0) / float(TOP * TOP), 1.0
    )
    out_ref[...] = (total - factor * pulled).astype(BF16)


def couple(own, lat, parts, matrix):
    return pl.pallas_call(
        couple_kernel,
        in_specs=[
            pl.BlockSpec(memory_space=pltpu.SMEM),
            pl.BlockSpec(memory_space=pltpu.SMEM),
            pl.BlockSpec(memory_space=pltpu.VMEM),
            pl.BlockSpec(memory_space=pltpu.VMEM),
        ],
        out_specs=pl.BlockSpec(memory_space=pltpu.VMEM),
        out_shape=jax.ShapeDtypeStruct((SHARE, K), BF16),
        compiler_params=pltpu.CompilerParams(vmem_limit_bytes=VMEM_LIMIT),
        cost_estimate=pl.CostEstimate(
            flops=2 * 416 * 128 * 128 * 6, bytes_accessed=1200000, transcendentals=0
        ),
        name="couple_levels",
    )(own, lat, parts, matrix)


def inverse_kernel(own_ref, block_ref, straight_ref, all_ref, out_ref, send_ref, held, rows):
    step = pl.program_id(0)

    @pl.when(step == 0)
    def _():
        held[:TOP, :] = jnp.zeros((TOP, K), BF16)
        held[TOP:, :] = all_ref[...]

    base = TOP + step * PAIR_ROWS
    unit = own_ref[2 * step] // UNIT
    size = TOP // GROUPS
    begin = block_ref[0] * size
    degree = begin + lax.broadcasted_iota(jnp.int32, (size, K), 0)
    for q in range(2):
        wave = own_ref[2 * step + q]
        start = base + UNIT if q == 0 else base - (UNITS - 1 - unit) * UNIT
        values = held[pl.ds(pl.multiple_of(start, UNIT), TOP), :]
        back = jnp.dot(straight_ref[q], values, preferred_element_type=F32)
        back = back * jnp.where(wave == 0, 1.0, 2.0)
        for li in range(ROWS):
            at = (2 * step + q) * ROWS + li
            rows[pl.ds(at, WAVES, stride=LINE), :] = back[li * WAVES : (li + 1) * WAVES]
        mine = held[pl.ds(pl.multiple_of(start + begin, UNIT), size), :]
        out_ref[q] = jnp.where(degree >= wave, mine.astype(F32), 0.0).astype(BF16)

    @pl.when(step == 4)
    def _():
        clear_spare(rows)
        tighten(rows, send_ref)


def inverse(own, block, straight, everything):
    return pl.pallas_call(
        inverse_kernel,
        grid=(5,),
        in_specs=[
            pl.BlockSpec(memory_space=pltpu.SMEM),
            pl.BlockSpec(memory_space=pltpu.SMEM),
            pl.BlockSpec((2, BAND, TOP), lambda i: (i, 0, 0)),
            pl.BlockSpec((PACKED, K), lambda i: (0, 0)),
        ],
        out_specs=[
            pl.BlockSpec((2, TOP // GROUPS, K), lambda i: (i, 0, 0)),
            pl.BlockSpec((WAVES * CHUNK, K), lambda i: (0, 0)),
        ],
        out_shape=[
            jax.ShapeDtypeStruct((SLOTS, TOP // GROUPS, K), BF16),
            jax.ShapeDtypeStruct((WAVES * CHUNK, K), BF16),
        ],
        scratch_shapes=[
            pltpu.VMEM((TOP + PACKED, K), BF16),
            pltpu.VMEM((WAVES * LINE, K), F32),
        ],
        compiler_params=params(),
        cost_estimate=pl.CostEstimate(
            flops=2 * 10 * 192 * 640 * 128, bytes_accessed=5000000, transcendentals=0
        ),
        name="inverse_sums",
    )(own, block, straight, everything)


def finish_kernel(
    got_ref, sign_ref, table_ref, out_ref, table, made, rows, left, loads, stores
):
    parts, _, _, block = table.shape
    lines = ROWS * FIELDS

    def load(part):
        at = pl.ds(pl.multiple_of(part * block, 128), block)
        return pltpu.make_async_copy(
            table_ref.at[:, :, at], table.at[part], loads.at[part]
        )

    def store(part, half):
        at = pl.ds(pl.multiple_of(half * HALF + part * block, 128), block)
        return pltpu.make_async_copy(
            made.at[part, half], out_ref.at[:, at], stores.at[part, half]
        )

    for part in range(parts):
        load(part).start()
    loosen(got_ref, rows)
    sign = sign_ref[...]
    for li in range(ROWS):
        values = jnp.concatenate(
            [
                rows[pl.ds(slot * ROWS + li, WAVES, stride=LINE), :]
                for slot in range(SLOTS)
            ],
            axis=0,
        )
        turned = values.T
        for half, one in enumerate((turned, turned * sign)):
            at = slice(half * lines + li * FIELDS, half * lines + (li + 1) * FIELDS)
            left[at, :TOP] = one[:FIELDS].astype(BF16)
            left[at, TOP:] = one[FIELDS:].astype(BF16)

    @pl.loop(0, parts)
    def _(part):
        load(part).wait()
        right = table[part].reshape(2 * TOP, block)
        both = jnp.dot(left[...], right, preferred_element_type=F32).astype(BF16)
        for half in range(2):
            made[part, half] = both[half * lines : (half + 1) * lines]
            store(part, half).start()
    for part in range(parts):
        for half in range(2):
            store(part, half).wait()


def finish(got, sign, table):
    parts = 5
    block = HALF // parts
    return pl.pallas_call(
        finish_kernel,
        in_specs=[
            pl.BlockSpec(memory_space=pltpu.VMEM),
            pl.BlockSpec(memory_space=pltpu.VMEM),
            pl.BlockSpec(memory_space=pl.ANY),
        ],
        out_specs=pl.BlockSpec(memory_space=pl.ANY),
        out_shape=jax.ShapeDtypeStruct((ROWS * FIELDS, NLON), BF16),
        scratch_shapes=[
            pltpu.VMEM((parts, 2, TOP, block), BF16),
            pltpu.VMEM((parts, 2, ROWS * FIELDS, block), BF16),
            pltpu.VMEM((WAVES * LINE, K), F32),
            pltpu.VMEM((2 * ROWS * FIELDS, 2 * TOP), BF16),
            pltpu.SemaphoreType.DMA((parts,)),
            pltpu.SemaphoreType.DMA((parts, 2)),
        ],
        compiler_params=pltpu.CompilerParams(vmem_limit_bytes=MIDDLE),
        cost_estimate=pl.CostEstimate(
            flops=2 * 192 * 2560 * 1280, bytes_accessed=6000000, transcendentals=0
        ),
        name="finish_rows",
    )(got, sign, table)


def coupling_matrix(couple_div, couple_temp):
    zero = jnp.zeros_like(couple_div)
    one = jnp.block([[zero, couple_temp.T], [couple_div.T, zero]])
    none = jnp.zeros_like(one)
    return jnp.block([[one, none], [none, one]])


def body(grid_in, legendre, wave_order, block_order, couple_div, couple_temp):
    lat = lax.axis_index("lat")
    wave = lax.axis_index("wave")
    send = forward(wave_order, grid_in.reshape(ROWS * FIELDS, NLON))
    swap = functools.partial(lax.all_to_all, split_axis=0, concat_axis=0, tiled=True)
    got = swap(send.reshape(WAVES, CHUNK, K), "wave")
    own = lax.dynamic_slice_in_dim(wave_order, wave * SLOTS, SLOTS)
    block = lax.dynamic_slice_in_dim(block_order, lat, 1)
    straight, turned = basis(own, legendre)
    waves = wave_order.reshape(WAVES, SLOTS).T.reshape(TOP)
    sign = (1 - 2 * (waves & 1)).astype(F32).reshape(1, TOP)
    table = inverse_table(jnp.broadcast_to(waves.astype(F32)[:, None], (TOP, 128)))
    matrix = coupling_matrix(couple_div, couple_temp)
    packed = partial_sums(own, turned, got.reshape(WAVES * CHUNK, K))
    parts = swap(packed.reshape(GROUPS, SHARE, K), "lat")
    spectral = couple(own, lat.reshape(1), parts, matrix)
    everything = lax.all_gather(spectral, "lat", axis=0, tiled=True)
    spectral_out, send = inverse(own, block, straight, everything)
    got = swap(send.reshape(WAVES, CHUNK, K), "wave")
    grid_out = finish(got.reshape(WAVES * CHUNK, K), sign, table)
    return spectral_out.transpose(1, 0, 2), grid_out.reshape(ROWS, FIELDS, NLON)


def solution(mesh):
    placed = (P(("lat", "wave"), None, None), P("wave", "lat", None), P(), P(), P(), P())
    return jax.shard_map(
        body,
        mesh=mesh,
        in_specs=placed,
        out_specs=(P("lat", "wave", None), P(("lat", "wave"), None, None)),
        check_vma=False,
    )
```

```python
import functools
import math

import jax
import jax.numpy as jnp
from jax import lax
from jax.experimental import pallas as pl
from jax.experimental.pallas import tpu as pltpu
from jax.sharding import PartitionSpec as P

F32 = jnp.float32
BF16 = jnp.bfloat16
NLON = 2560
HALF = NLON // 2
WAVES = 64
GROUPS = 8
SLOTS = 10
ROWS = 3
FIELDS = 64
K = 128
TOP = 640
BAND = 192
CHUNK = 32
LINE = CHUNK + 1
UNIT = 16
UNITS = TOP // UNIT
PAIR_ROWS = TOP + UNIT
PACKED = 3328
SHARE = PACKED // GROUPS
VMEM_LIMIT = 24 * 1024 * 1024
LARGE = 58 * 1024 * 1024
MIDDLE = 52 * 1024 * 1024


def params(limit=VMEM_LIMIT):
    return pltpu.CompilerParams(
        dimension_semantics=("arbitrary",), vmem_limit_bytes=limit
    )


def cos_sin(phase):
    quarter = (
        (phase >= 320.0).astype(F32)
        + (phase >= 960.0).astype(F32)
        + (phase >= 1600.0).astype(F32)
        + (phase >= 2240.0).astype(F32)
    )
    x = (phase - 640.0 * quarter) * (2.0 * math.pi / NLON)
    y = x * x
    s = x * (
        1.0 + y * (-1.0 / 6 + y * (1.0 / 120 + y * (-1.0 / 5040 + y * (1.0 / 362880))))
    )
    c = 1.0 + y * (
        -0.5 + y * (1.0 / 24 + y * (-1.0 / 720 + y * (1.0 / 40320 + y * (-1.0 / 3628800))))
    )
    odd = (quarter == 1.0) | (quarter == 3.0)
    cos = jnp.where(odd, s, c)
    sin = jnp.where(odd, c, s)
    cos = jnp.where((quarter == 1.0) | (quarter == 2.0), -cos, cos)
    sin = jnp.where((quarter == 2.0) | (quarter == 3.0), -sin, sin)
    return cos, sin


def phase_of(product):
    return product - NLON * jnp.floor((product + 0.5) * (1.0 / NLON))


def forward_kernel(waves_ref, grid_ref, send_ref, grid, near, far, lines, rows, sem):
    step = pl.program_id(0)

    @pl.when(step == 0)
    def _():
        loads = [
            pltpu.make_async_copy(
                grid_ref.at[:, pl.ds(half * HALF, HALF)],
                grid.at[pl.ds(half * ROWS * FIELDS, ROWS * FIELDS)],
                sem.at[half],
            )
            for half in range(2)
        ]
        for load in loads:
            load.start()
        waves = waves_ref[...].astype(F32).reshape(1, TOP)
        down = lax.broadcasted_iota(jnp.int32, (128, TOP), 0).astype(F32)
        c, s = cos_sin(phase_of(waves * down))
        near[0] = c
        near[1] = s
        c, s = cos_sin(phase_of(waves * (down[:16] * 128.0)))
        factor = 1.0 / math.sqrt(NLON)
        far[0] = c * factor
        far[1] = s * factor
        for load in loads:
            load.wait()

    at = pl.ds(pl.multiple_of(step * 128, 128), 128)
    near_c = near[0, :, at]
    near_s = near[1, :, at]
    far_c = far[0, :, at]
    far_s = far[1, :, at]
    made = jnp.zeros((2 * ROWS * FIELDS, 256), F32)
    for a in range(0, HALF // 128, 2):
        right = []
        for b in (a, a + 1):
            ca = far_c[b : b + 1]
            sa = far_s[b : b + 1]
            c = ca * near_c - sa * near_s
            s = -(sa * near_c) - ca * near_s
            right.append(jnp.concatenate([c, s], axis=1).astype(BF16))
        made = made + jnp.dot(
            grid[:, a * 128 : (a + 2) * 128],
            jnp.concatenate(right, axis=0),
            preferred_element_type=F32,
        )
    sign = jnp.where(far_c[HALF // 128 : HALF // 128 + 1] > 0.0, 1.0, -1.0)
    sign = jnp.concatenate([sign, sign], axis=1)
    made = made[: ROWS * FIELDS] + sign * made[ROWS * FIELDS :]
    for li in range(ROWS):
        one = made[li * FIELDS : (li + 1) * FIELDS]
        lines[li, at, :] = jnp.concatenate([one[:, :128], one[:, 128:]], axis=0).T

    @pl.when(step == TOP // 128 - 1)
    def _():
        for li in range(ROWS):
            for slot in range(SLOTS):
                rows[pl.ds(slot * ROWS + li, WAVES, stride=LINE), :] = lines[
                    li, pl.ds(slot, WAVES, stride=SLOTS), :
                ]
        clear_spare(rows)
        tighten(rows, send_ref)


def clear_spare(rows):
    for row in range(SLOTS * ROWS, CHUNK):
        rows[pl.ds(row, WAVES, stride=LINE), :] = jnp.zeros((WAVES, K), F32)


def tighten(rows, out):
    for wave in range(WAVES):
        out[wave * CHUNK : (wave + 1) * CHUNK, :] = rows[
            wave * LINE : wave * LINE + CHUNK, :
        ].astype(BF16)


def loosen(got, rows):
    for wave in range(WAVES):
        rows[wave * LINE : wave * LINE + CHUNK, :] = got[
            wave * CHUNK : (wave + 1) * CHUNK, :
        ].astype(F32)


def forward(waves, grid):
    return pl.pallas_call(
        forward_kernel,
        grid=(TOP // 128,),
        in_specs=[
            pl.BlockSpec((TOP,), lambda i: (0,)),
            pl.BlockSpec(memory_space=pl.ANY),
        ],
        out_specs=pl.BlockSpec((WAVES * CHUNK, K), lambda i: (0, 0)),
        out_shape=jax.ShapeDtypeStruct((WAVES * CHUNK, K), BF16),
        scratch_shapes=[
            pltpu.VMEM((2 * ROWS * FIELDS, HALF), BF16),
            pltpu.VMEM((2, 128, TOP), F32),
            pltpu.VMEM((2, 16, TOP), F32),
            pltpu.VMEM((ROWS, TOP, K), F32),
            pltpu.VMEM((WAVES * LINE, K), F32),
            pltpu.SemaphoreType.DMA((2,)),
        ],
        compiler_params=params(LARGE),
        cost_estimate=pl.CostEstimate(
            flops=2 * 192 * 2560 * 1280, bytes_accessed=2000000, transcendentals=0
        ),
        name="forward_rows",
    )(waves, grid)


def table_kernel(waves_ref, table_ref):
    waves = waves_ref[...]
    lanes = lax.broadcasted_iota(jnp.int32, waves.shape, 1).astype(F32)
    near_c, near_s = cos_sin(phase_of(waves * lanes))
    far_c, far_s = cos_sin(phase_of(waves * (lanes * 128.0)))
    factor = 1.0 / math.sqrt(NLON)
    far_c = far_c * factor
    far_s = far_s * factor
    for a in range(HALF // 128):
        ca = far_c[:, a : a + 1]
        sa = far_s[:, a : a + 1]
        at = slice(a * 128, (a + 1) * 128)
        table_ref[0, :, at] = (ca * near_c - sa * near_s).astype(BF16)
        table_ref[1, :, at] = (-(sa * near_c) - ca * near_s).astype(BF16)


def inverse_table(waves):
    return pl.pallas_call(
        table_kernel,
        grid=(5,),
        in_specs=[pl.BlockSpec((128, 128), lambda i: (i, 0))],
        out_specs=pl.BlockSpec((2, 128, HALF), lambda i: (0, i, 0)),
        out_shape=jax.ShapeDtypeStruct((2, TOP, HALF), BF16),
        compiler_params=params(LARGE),
        cost_estimate=pl.CostEstimate(
            flops=30000000, bytes_accessed=6000000, transcendentals=0
        ),
        name="inverse_table",
    )(waves)


def basis_kernel(own_ref, leg_ref, straight_ref, turned_ref, rows, joined):
    wave = own_ref[pl.program_id(0)]
    for b in range(TOP // 128):
        at = slice(b * 128, (b + 1) * 128)
        degree = b * 128 + lax.broadcasted_iota(jnp.int32, (BAND, 128), 1)
        rows[b] = jnp.where(degree >= wave, leg_ref[0, :, at].astype(F32), 0.0)
        for li in range(ROWS):
            joined[li * WAVES : (li + 1) * WAVES, at] = rows[
                b, pl.ds(li, WAVES, stride=ROWS), :
            ]
    straight_ref[0] = joined[...].astype(BF16)
    turned_ref[0] = joined[...].T.astype(BF16)


def basis(own, legendre):
    return pl.pallas_call(
        basis_kernel,
        grid=(SLOTS,),
        in_specs=[
            pl.BlockSpec(memory_space=pltpu.SMEM),
            pl.BlockSpec((1, BAND, TOP), lambda i: (i, 0, 0)),
        ],
        out_specs=[
            pl.BlockSpec((1, BAND, TOP), lambda i: (i, 0, 0)),
            pl.BlockSpec((1, TOP, BAND), lambda i: (i, 0, 0)),
        ],
        out_shape=[
            jax.ShapeDtypeStruct((SLOTS, BAND, TOP), BF16),
            jax.ShapeDtypeStruct((SLOTS, TOP, BAND), BF16),
        ],
        scratch_shapes=[
            pltpu.VMEM((TOP // 128, BAND, 128), F32),
            pltpu.VMEM((BAND, TOP), F32),
        ],
        compiler_params=params(),
        cost_estimate=pl.CostEstimate(
            flops=0, bytes_accessed=30000000, transcendentals=0
        ),
        name="basis_rows",
    )(own, legendre)


def partial_kernel(own_ref, turned_ref, got_ref, packed_ref, rows, held):
    step = pl.program_id(0)
    pair = 4 - step

    @pl.when(step == 0)
    def _():
        loosen(got_ref, rows)
        held[TOP + 5 * PAIR_ROWS :, :] = jnp.zeros((PACKED - 5 * PAIR_ROWS, K), BF16)

    def product(q):
        slot = 2 * pair + q
        values = jnp.concatenate(
            [
                rows[pl.ds(slot * ROWS + li, WAVES, stride=LINE), :]
                for li in range(ROWS)
            ],
            axis=0,
        ).astype(BF16)
        return jnp.dot(turned_ref[q], values, preferred_element_type=F32).astype(BF16)

    unit = own_ref[2 * pair] // UNIT
    base = TOP + pair * PAIR_ROWS
    held[pl.ds(pl.multiple_of(base + UNIT, UNIT), TOP), :] = product(0)
    at = pl.multiple_of(base - (UNITS - 1 - unit) * UNIT, UNIT)
    held[pl.ds(at, TOP), :] = product(1)

    @pl.when(step == 4)
    def _():
        packed_ref[...] = held[TOP:, :]


def partial_sums(own, turned, got):
    return pl.pallas_call(
        partial_kernel,
        grid=(5,),
        in_specs=[
            pl.BlockSpec(memory_space=pltpu.SMEM),
            pl.BlockSpec((2, TOP, BAND), lambda i: (4 - i, 0, 0)),
            pl.BlockSpec((WAVES * CHUNK, K), lambda i: (0, 0)),
        ],
        out_specs=pl.BlockSpec((PACKED, K), lambda i: (0, 0)),
        out_shape=jax.ShapeDtypeStruct((PACKED, K), BF16),
        scratch_shapes=[
            pltpu.VMEM((WAVES * LINE, K), F32),
            pltpu.VMEM((TOP + PACKED, K), BF16),
        ],
        compiler_params=params(),
        cost_estimate=pl.CostEstimate(
            flops=2 * 10 * 192 * 640 * 128, bytes_accessed=5000000, transcendentals=0
        ),
        name="partial_sums",
    )(own, turned, got)


def couple_kernel(own_ref, lat_ref, parts_ref, couple_ref, out_ref):
    total = parts_ref[0].astype(F32)
    for g in range(1, GROUPS):
        total = total + parts_ref[g].astype(F32)
    pulled = jnp.dot(
        total,
        couple_ref[...],
        preferred_element_type=F32,
        precision=lax.Precision.HIGHEST,
    )
    position = lat_ref[0] * SHARE + lax.broadcasted_iota(jnp.int32, (SHARE, K), 0)
    degree = jnp.zeros((SHARE, K), jnp.int32)
    for pair in range(SLOTS // 2):
        unit = own_ref[2 * pair] // UNIT
        inside = position - pair * PAIR_ROWS
        shift = jnp.where(inside >= (unit + 1) * UNIT, -UNIT, (UNITS - 1 - unit) * UNIT)
        degree = jnp.where(inside >= 0, inside + shift, degree)
    degree = degree.astype(F32)
    column = lax.broadcasted_iota(jnp.int32, (SHARE, K), 1)
    factor = jnp.where(
        (column & 63) < 32, degree * (degree + 1.0) / float(TOP * TOP), 1.0
    )
    out_ref[...] = (total - factor * pulled).astype(BF16)


def couple(own, lat, parts, matrix):
    return pl.pallas_call(
        couple_kernel,
        in_specs=[
            pl.BlockSpec(memory_space=pltpu.SMEM),
            pl.BlockSpec(memory_space=pltpu.SMEM),
            pl.BlockSpec(memory_space=pltpu.VMEM),
            pl.BlockSpec(memory_space=pltpu.VMEM),
        ],
        out_specs=pl.BlockSpec(memory_space=pltpu.VMEM),
        out_shape=jax.ShapeDtypeStruct((SHARE, K), BF16),
        compiler_params=pltpu.CompilerParams(vmem_limit_bytes=VMEM_LIMIT),
        cost_estimate=pl.CostEstimate(
            flops=2 * 416 * 128 * 128 * 6, bytes_accessed=1200000, transcendentals=0
        ),
        name="couple_levels",
    )(own, lat, parts, matrix)


def inverse_kernel(own_ref, block_ref, straight_ref, all_ref, out_ref, send_ref, held, rows):
    step = pl.program_id(0)

    @pl.when(step == 0)
    def _():
        held[:TOP, :] = jnp.zeros((TOP, K), BF16)
        held[TOP:, :] = all_ref[...]

    base = TOP + step * PAIR_ROWS
    unit = own_ref[2 * step] // UNIT
    size = TOP // GROUPS
    begin = block_ref[0] * size
    degree = begin + lax.broadcasted_iota(jnp.int32, (size, K), 0)
    for q in range(2):
        wave = own_ref[2 * step + q]
        start = base + UNIT if q == 0 else base - (UNITS - 1 - unit) * UNIT
        values = held[pl.ds(pl.multiple_of(start, UNIT), TOP), :]
        back = jnp.dot(straight_ref[q], values, preferred_element_type=F32)
        back = back * jnp.where(wave == 0, 1.0, 2.0)
        for li in range(ROWS):
            at = (2 * step + q) * ROWS + li
            rows[pl.ds(at, WAVES, stride=LINE), :] = back[li * WAVES : (li + 1) * WAVES]
        mine = held[pl.ds(pl.multiple_of(start + begin, UNIT), size), :]
        out_ref[q] = jnp.where(degree >= wave, mine.astype(F32), 0.0).astype(BF16)

    @pl.when(step == 4)
    def _():
        clear_spare(rows)
        tighten(rows, send_ref)


def inverse(own, block, straight, everything):
    return pl.pallas_call(
        inverse_kernel,
        grid=(5,),
        in_specs=[
            pl.BlockSpec(memory_space=pltpu.SMEM),
            pl.BlockSpec(memory_space=pltpu.SMEM),
            pl.BlockSpec((2, BAND, TOP), lambda i: (i, 0, 0)),
            pl.BlockSpec((PACKED, K), lambda i: (0, 0)),
        ],
        out_specs=[
            pl.BlockSpec((2, TOP // GROUPS, K), lambda i: (i, 0, 0)),
            pl.BlockSpec((WAVES * CHUNK, K), lambda i: (0, 0)),
        ],
        out_shape=[
            jax.ShapeDtypeStruct((SLOTS, TOP // GROUPS, K), BF16),
            jax.ShapeDtypeStruct((WAVES * CHUNK, K), BF16),
        ],
        scratch_shapes=[
            pltpu.VMEM((TOP + PACKED, K), BF16),
            pltpu.VMEM((WAVES * LINE, K), F32),
        ],
        compiler_params=params(),
        cost_estimate=pl.CostEstimate(
            flops=2 * 10 * 192 * 640 * 128, bytes_accessed=5000000, transcendentals=0
        ),
        name="inverse_sums",
    )(own, block, straight, everything)


def finish_kernel(
    got_ref, sign_ref, table_ref, out_ref, table, made, rows, left, loads, stores
):
    parts, _, _, block = table.shape
    lines = ROWS * FIELDS

    def load(part):
        at = pl.ds(pl.multiple_of(part * block, 128), block)
        return pltpu.make_async_copy(
            table_ref.at[:, :, at], table.at[part], loads.at[part]
        )

    def store(part, half):
        at = pl.ds(pl.multiple_of(half * HALF + part * block, 128), block)
        return pltpu.make_async_copy(
            made.at[part, half], out_ref.at[:, at], stores.at[part, half]
        )

    for part in range(parts):
        load(part).start()
    loosen(got_ref, rows)
    sign = sign_ref[...]
    for li in range(ROWS):
        values = jnp.concatenate(
            [
                rows[pl.ds(slot * ROWS + li, WAVES, stride=LINE), :]
                for slot in range(SLOTS)
            ],
            axis=0,
        )
        turned = values.T
        for half, one in enumerate((turned, turned * sign)):
            at = slice(half * lines + li * FIELDS, half * lines + (li + 1) * FIELDS)
            left[at, :TOP] = one[:FIELDS].astype(BF16)
            left[at, TOP:] = one[FIELDS:].astype(BF16)

    @pl.loop(0, parts)
    def _(part):
        load(part).wait()
        right = table[part].reshape(2 * TOP, block)
        both = jnp.dot(left[...], right, preferred_element_type=F32).astype(BF16)
        for half in range(2):
            made[part, half] = both[half * lines : (half + 1) * lines]
            store(part, half).start()
    for part in range(parts):
        for half in range(2):
            store(part, half).wait()


def finish(got, sign, table):
    parts = 5
    block = HALF // parts
    return pl.pallas_call(
        finish_kernel,
        in_specs=[
            pl.BlockSpec(memory_space=pltpu.VMEM),
            pl.BlockSpec(memory_space=pltpu.VMEM),
            pl.BlockSpec(memory_space=pl.ANY),
        ],
        out_specs=pl.BlockSpec(memory_space=pl.ANY),
        out_shape=jax.ShapeDtypeStruct((ROWS * FIELDS, NLON), BF16),
        scratch_shapes=[
            pltpu.VMEM((parts, 2, TOP, block), BF16),
            pltpu.VMEM((parts, 2, ROWS * FIELDS, block), BF16),
            pltpu.VMEM((WAVES * LINE, K), F32),
            pltpu.VMEM((2 * ROWS * FIELDS, 2 * TOP), BF16),
            pltpu.SemaphoreType.DMA((parts,)),
            pltpu.SemaphoreType.DMA((parts, 2)),
        ],
        compiler_params=pltpu.CompilerParams(vmem_limit_bytes=MIDDLE),
        cost_estimate=pl.CostEstimate(
            flops=2 * 192 * 2560 * 1280, bytes_accessed=6000000, transcendentals=0
        ),
        name="finish_rows",
    )(got, sign, table)


def coupling_matrix(couple_div, couple_temp):
    zero = jnp.zeros_like(couple_div)
    one = jnp.block([[zero, couple_temp.T], [couple_div.T, zero]])
    none = jnp.zeros_like(one)
    return jnp.block([[one, none], [none, one]])


def body(grid_in, legendre, wave_order, block_order, couple_div, couple_temp):
    lat = lax.axis_index("lat")
    wave = lax.axis_index("wave")
    send = forward(wave_order, grid_in.reshape(ROWS * FIELDS, NLON))
    swap = functools.partial(lax.all_to_all, split_axis=0, concat_axis=0, tiled=True)
    got = swap(send.reshape(WAVES, CHUNK, K), "wave")
    own = lax.dynamic_slice_in_dim(wave_order, wave * SLOTS, SLOTS)
    block = lax.dynamic_slice_in_dim(block_order, lat, 1)
    straight, turned = basis(own, legendre)
    waves = wave_order.reshape(WAVES, SLOTS).T.reshape(TOP)
    sign = (1 - 2 * (waves & 1)).astype(F32).reshape(1, TOP)
    table = inverse_table(jnp.broadcast_to(waves.astype(F32)[:, None], (TOP, 128)))
    matrix = coupling_matrix(couple_div, couple_temp)
    turned, straight, table, sign, matrix, block, own, lat = lax.optimization_barrier(
        (turned, straight, table, sign, matrix, block, own, lat.reshape(1))
    )
    packed = partial_sums(own, turned, got.reshape(WAVES * CHUNK, K))
    parts = swap(packed.reshape(GROUPS, SHARE, K), "lat")
    spectral = couple(own, lat, parts, matrix)
    everything = lax.all_gather(spectral, "lat", axis=0, tiled=True)
    spectral_out, send = inverse(own, block, straight, everything)
    got = swap(send.reshape(WAVES, CHUNK, K), "wave")
    grid_out = finish(got.reshape(WAVES * CHUNK, K), sign, table)
    return spectral_out.transpose(1, 0, 2), grid_out.reshape(ROWS, FIELDS, NLON)


def solution(mesh):
    placed = (P(("lat", "wave"), None, None), P("wave", "lat", None), P(), P(), P(), P())
    return jax.shard_map(
        body,
        mesh=mesh,
        in_specs=placed,
        out_specs=(P("lat", "wave", None), P(("lat", "wave"), None, None)),
        check_vma=False,
    )
```

```python
import functools
import math

import jax
import jax.numpy as jnp
from jax import lax
from jax.experimental import pallas as pl
from jax.experimental.pallas import tpu as pltpu
from jax.sharding import PartitionSpec as P

F32 = jnp.float32
BF16 = jnp.bfloat16
NLON = 2560
HALF = NLON // 2
WAVES = 64
GROUPS = 8
SLOTS = 10
ROWS = 3
FIELDS = 64
K = 128
TOP = 640
BAND = 192
CHUNK = 32
LINE = CHUNK + 1
UNIT = 16
UNITS = TOP // UNIT
PAIR_ROWS = TOP + UNIT
PACKED = 3328
SHARE = PACKED // GROUPS
VMEM_LIMIT = 24 * 1024 * 1024
LARGE = 58 * 1024 * 1024
MIDDLE = 40 * 1024 * 1024


def params(limit=VMEM_LIMIT):
    return pltpu.CompilerParams(
        dimension_semantics=("arbitrary",), vmem_limit_bytes=limit
    )


def cos_sin(phase):
    quarter = (
        (phase >= 320.0).astype(F32)
        + (phase >= 960.0).astype(F32)
        + (phase >= 1600.0).astype(F32)
        + (phase >= 2240.0).astype(F32)
    )
    x = (phase - 640.0 * quarter) * (2.0 * math.pi / NLON)
    y = x * x
    s = x * (
        1.0 + y * (-1.0 / 6 + y * (1.0 / 120 + y * (-1.0 / 5040 + y * (1.0 / 362880))))
    )
    c = 1.0 + y * (
        -0.5 + y * (1.0 / 24 + y * (-1.0 / 720 + y * (1.0 / 40320 + y * (-1.0 / 3628800))))
    )
    odd = (quarter == 1.0) | (quarter == 3.0)
    cos = jnp.where(odd, s, c)
    sin = jnp.where(odd, c, s)
    cos = jnp.where((quarter == 1.0) | (quarter == 2.0), -cos, cos)
    sin = jnp.where((quarter == 2.0) | (quarter == 3.0), -sin, sin)
    return cos, sin


def phase_of(product):
    return product - NLON * jnp.floor((product + 0.5) * (1.0 / NLON))


def forward_kernel(waves_ref, grid_ref, send_ref, grid, near, far, lines, rows, sem):
    step = pl.program_id(0)

    @pl.when(step == 0)
    def _():
        loads = [
            pltpu.make_async_copy(
                grid_ref.at[:, pl.ds(half * HALF, HALF)],
                grid.at[pl.ds(half * ROWS * FIELDS, ROWS * FIELDS)],
                sem.at[half],
            )
            for half in range(2)
        ]
        for load in loads:
            load.start()
        waves = waves_ref[...].astype(F32).reshape(1, TOP)
        down = lax.broadcasted_iota(jnp.int32, (128, TOP), 0).astype(F32)
        c, s = cos_sin(phase_of(waves * down))
        near[0] = c
        near[1] = s
        c, s = cos_sin(phase_of(waves * (down[:16] * 128.0)))
        factor = 1.0 / math.sqrt(NLON)
        far[0] = c * factor
        far[1] = s * factor
        for load in loads:
            load.wait()

    at = pl.ds(pl.multiple_of(step * 128, 128), 128)
    near_c = near[0, :, at]
    near_s = near[1, :, at]
    far_c = far[0, :, at]
    far_s = far[1, :, at]
    made = jnp.zeros((2 * ROWS * FIELDS, 256), F32)
    for a in range(0, HALF // 128, 2):
        right = []
        for b in (a, a + 1):
            ca = far_c[b : b + 1]
            sa = far_s[b : b + 1]
            c = ca * near_c - sa * near_s
            s = -(sa * near_c) - ca * near_s
            right.append(jnp.concatenate([c, s], axis=1).astype(BF16))
        made = made + jnp.dot(
            grid[:, a * 128 : (a + 2) * 128],
            jnp.concatenate(right, axis=0),
            preferred_element_type=F32,
        )
    sign = jnp.where(far_c[HALF // 128 : HALF // 128 + 1] > 0.0, 1.0, -1.0)
    sign = jnp.concatenate([sign, sign], axis=1)
    made = made[: ROWS * FIELDS] + sign * made[ROWS * FIELDS :]
    for li in range(ROWS):
        one = made[li * FIELDS : (li + 1) * FIELDS]
        lines[li, at, :] = jnp.concatenate([one[:, :128], one[:, 128:]], axis=0).T

    @pl.when(step == TOP // 128 - 1)
    def _():
        for li in range(ROWS):
            for slot in range(SLOTS):
                rows[pl.ds(slot * ROWS + li, WAVES, stride=LINE), :] = lines[
                    li, pl.ds(slot, WAVES, stride=SLOTS), :
                ]
        clear_spare(rows)
        tighten(rows, send_ref)


def clear_spare(rows):
    for row in range(SLOTS * ROWS, CHUNK):
        rows[pl.ds(row, WAVES, stride=LINE), :] = jnp.zeros((WAVES, K), F32)


def tighten(rows, out):
    for wave in range(WAVES):
        out[wave * CHUNK : (wave + 1) * CHUNK, :] = rows[
            wave * LINE : wave * LINE + CHUNK, :
        ].astype(BF16)


def loosen(got, rows):
    for wave in range(WAVES):
        rows[wave * LINE : wave * LINE + CHUNK, :] = got[
            wave * CHUNK : (wave + 1) * CHUNK, :
        ].astype(F32)


def forward(waves, grid):
    return pl.pallas_call(
        forward_kernel,
        grid=(TOP // 128,),
        in_specs=[
            pl.BlockSpec((TOP,), lambda i: (0,)),
            pl.BlockSpec(memory_space=pl.ANY),
        ],
        out_specs=pl.BlockSpec((WAVES * CHUNK, K), lambda i: (0, 0)),
        out_shape=jax.ShapeDtypeStruct((WAVES * CHUNK, K), BF16),
        scratch_shapes=[
            pltpu.VMEM((2 * ROWS * FIELDS, HALF), BF16),
            pltpu.VMEM((2, 128, TOP), F32),
            pltpu.VMEM((2, 16, TOP), F32),
            pltpu.VMEM((ROWS, TOP, K), F32),
            pltpu.VMEM((WAVES * LINE, K), F32),
            pltpu.SemaphoreType.DMA((2,)),
        ],
        compiler_params=params(LARGE),
        cost_estimate=pl.CostEstimate(
            flops=2 * 192 * 2560 * 1280, bytes_accessed=2000000, transcendentals=0
        ),
        name="forward_rows",
    )(waves, grid)


def table_kernel(waves_ref, table_ref):
    waves = waves_ref[...]
    lanes = lax.broadcasted_iota(jnp.int32, waves.shape, 1).astype(F32)
    near_c, near_s = cos_sin(phase_of(waves * lanes))
    far_c, far_s = cos_sin(phase_of(waves * (lanes * 128.0)))
    factor = 1.0 / math.sqrt(NLON)
    far_c = far_c * factor
    far_s = far_s * factor
    for a in range(HALF // 128):
        ca = far_c[:, a : a + 1]
        sa = far_s[:, a : a + 1]
        at = slice(a * 128, (a + 1) * 128)
        table_ref[0, :, at] = (ca * near_c - sa * near_s).astype(BF16)
        table_ref[1, :, at] = (-(sa * near_c) - ca * near_s).astype(BF16)


def inverse_table(waves):
    return pl.pallas_call(
        table_kernel,
        grid=(5,),
        in_specs=[pl.BlockSpec((128, 128), lambda i: (i, 0))],
        out_specs=pl.BlockSpec((2, 128, HALF), lambda i: (0, i, 0)),
        out_shape=jax.ShapeDtypeStruct((2, TOP, HALF), BF16),
        compiler_params=params(LARGE),
        cost_estimate=pl.CostEstimate(
            flops=30000000, bytes_accessed=6000000, transcendentals=0
        ),
        name="inverse_table",
    )(waves)


def basis_kernel(own_ref, leg_ref, straight_ref, turned_ref, rows, joined):
    wave = own_ref[pl.program_id(0)]
    for b in range(TOP // 128):
        at = slice(b * 128, (b + 1) * 128)
        degree = b * 128 + lax.broadcasted_iota(jnp.int32, (BAND, 128), 1)
        rows[b] = jnp.where(degree >= wave, leg_ref[0, :, at].astype(F32), 0.0)
        for li in range(ROWS):
            joined[li * WAVES : (li + 1) * WAVES, at] = rows[
                b, pl.ds(li, WAVES, stride=ROWS), :
            ]
    straight_ref[0] = joined[...].astype(BF16)
    turned_ref[0] = joined[...].T.astype(BF16)


def basis(own, legendre):
    return pl.pallas_call(
        basis_kernel,
        grid=(SLOTS,),
        in_specs=[
            pl.BlockSpec(memory_space=pltpu.SMEM),
            pl.BlockSpec((1, BAND, TOP), lambda i: (i, 0, 0)),
        ],
        out_specs=[
            pl.BlockSpec((1, BAND, TOP), lambda i: (i, 0, 0)),
            pl.BlockSpec((1, TOP, BAND), lambda i: (i, 0, 0)),
        ],
        out_shape=[
            jax.ShapeDtypeStruct((SLOTS, BAND, TOP), BF16),
            jax.ShapeDtypeStruct((SLOTS, TOP, BAND), BF16),
        ],
        scratch_shapes=[
            pltpu.VMEM((TOP // 128, BAND, 128), F32),
            pltpu.VMEM((BAND, TOP), F32),
        ],
        compiler_params=params(),
        cost_estimate=pl.CostEstimate(
            flops=0, bytes_accessed=30000000, transcendentals=0
        ),
        name="basis_rows",
    )(own, legendre)


def partial_kernel(own_ref, turned_ref, got_ref, packed_ref, rows, held):
    step = pl.program_id(0)
    pair = 4 - step

    @pl.when(step == 0)
    def _():
        loosen(got_ref, rows)
        held[TOP + 5 * PAIR_ROWS :, :] = jnp.zeros((PACKED - 5 * PAIR_ROWS, K), BF16)

    def product(q):
        slot = 2 * pair + q
        values = jnp.concatenate(
            [
                rows[pl.ds(slot * ROWS + li, WAVES, stride=LINE), :]
                for li in range(ROWS)
            ],
            axis=0,
        ).astype(BF16)
        return jnp.dot(turned_ref[q], values, preferred_element_type=F32).astype(BF16)

    unit = own_ref[2 * pair] // UNIT
    base = TOP + pair * PAIR_ROWS
    held[pl.ds(pl.multiple_of(base + UNIT, UNIT), TOP), :] = product(0)
    at = pl.multiple_of(base - (UNITS - 1 - unit) * UNIT, UNIT)
    held[pl.ds(at, TOP), :] = product(1)

    @pl.when(step == 4)
    def _():
        packed_ref[...] = held[TOP:, :]


def partial_sums(own, turned, got):
    return pl.pallas_call(
        partial_kernel,
        grid=(5,),
        in_specs=[
            pl.BlockSpec(memory_space=pltpu.SMEM),
            pl.BlockSpec((2, TOP, BAND), lambda i: (4 - i, 0, 0)),
            pl.BlockSpec((WAVES * CHUNK, K), lambda i: (0, 0)),
        ],
        out_specs=pl.BlockSpec((PACKED, K), lambda i: (0, 0)),
        out_shape=jax.ShapeDtypeStruct((PACKED, K), BF16),
        scratch_shapes=[
            pltpu.VMEM((WAVES * LINE, K), F32),
            pltpu.VMEM((TOP + PACKED, K), BF16),
        ],
        compiler_params=params(),
        cost_estimate=pl.CostEstimate(
            flops=2 * 10 * 192 * 640 * 128, bytes_accessed=5000000, transcendentals=0
        ),
        name="partial_sums",
    )(own, turned, got)


def couple_kernel(own_ref, lat_ref, parts_ref, couple_ref, out_ref):
    total = parts_ref[0].astype(F32)
    for g in range(1, GROUPS):
        total = total + parts_ref[g].astype(F32)
    pulled = jnp.dot(
        total,
        couple_ref[...],
        preferred_element_type=F32,
        precision=lax.Precision.HIGHEST,
    )
    position = lat_ref[0] * SHARE + lax.broadcasted_iota(jnp.int32, (SHARE, K), 0)
    degree = jnp.zeros((SHARE, K), jnp.int32)
    for pair in range(SLOTS // 2):
        unit = own_ref[2 * pair] // UNIT
        inside = position - pair * PAIR_ROWS
        shift = jnp.where(inside >= (unit + 1) * UNIT, -UNIT, (UNITS - 1 - unit) * UNIT)
        degree = jnp.where(inside >= 0, inside + shift, degree)
    degree = degree.astype(F32)
    column = lax.broadcasted_iota(jnp.int32, (SHARE, K), 1)
    factor = jnp.where(
        (column & 63) < 32, degree * (degree + 1.0) / float(TOP * TOP), 1.0
    )
    out_ref[...] = (total - factor * pulled).astype(BF16)


def couple(own, lat, parts, matrix):
    return pl.pallas_call(
        couple_kernel,
        in_specs=[
            pl.BlockSpec(memory_space=pltpu.SMEM),
            pl.BlockSpec(memory_space=pltpu.SMEM),
            pl.BlockSpec(memory_space=pltpu.VMEM),
            pl.BlockSpec(memory_space=pltpu.VMEM),
        ],
        out_specs=pl.BlockSpec(memory_space=pltpu.VMEM),
        out_shape=jax.ShapeDtypeStruct((SHARE, K), BF16),
        compiler_params=pltpu.CompilerParams(vmem_limit_bytes=VMEM_LIMIT),
        cost_estimate=pl.CostEstimate(
            flops=2 * 416 * 128 * 128 * 6, bytes_accessed=1200000, transcendentals=0
        ),
        name="couple_levels",
    )(own, lat, parts, matrix)


def inverse_kernel(own_ref, block_ref, straight_ref, all_ref, out_ref, send_ref, held, rows):
    step = pl.program_id(0)

    @pl.when(step == 0)
    def _():
        held[:TOP, :] = jnp.zeros((TOP, K), BF16)
        held[TOP:, :] = all_ref[...]

    base = TOP + step * PAIR_ROWS
    unit = own_ref[2 * step] // UNIT
    size = TOP // GROUPS
    begin = block_ref[0] * size
    degree = begin + lax.broadcasted_iota(jnp.int32, (size, K), 0)
    for q in range(2):
        wave = own_ref[2 * step + q]
        start = base + UNIT if q == 0 else base - (UNITS - 1 - unit) * UNIT
        values = held[pl.ds(pl.multiple_of(start, UNIT), TOP), :]
        back = jnp.dot(straight_ref[q], values, preferred_element_type=F32)
        back = back * jnp.where(wave == 0, 1.0, 2.0)
        for li in range(ROWS):
            at = (2 * step + q) * ROWS + li
            rows[pl.ds(at, WAVES, stride=LINE), :] = back[li * WAVES : (li + 1) * WAVES]
        mine = held[pl.ds(pl.multiple_of(start + begin, UNIT), size), :]
        out_ref[q] = jnp.where(degree >= wave, mine.astype(F32), 0.0).astype(BF16)

    @pl.when(step == 4)
    def _():
        clear_spare(rows)
        tighten(rows, send_ref)


def inverse(own, block, straight, everything):
    return pl.pallas_call(
        inverse_kernel,
        grid=(5,),
        in_specs=[
            pl.BlockSpec(memory_space=pltpu.SMEM),
            pl.BlockSpec(memory_space=pltpu.SMEM),
            pl.BlockSpec((2, BAND, TOP), lambda i: (i, 0, 0)),
            pl.BlockSpec((PACKED, K), lambda i: (0, 0)),
        ],
        out_specs=[
            pl.BlockSpec((2, TOP // GROUPS, K), lambda i: (i, 0, 0)),
            pl.BlockSpec((WAVES * CHUNK, K), lambda i: (0, 0)),
        ],
        out_shape=[
            jax.ShapeDtypeStruct((SLOTS, TOP // GROUPS, K), BF16),
            jax.ShapeDtypeStruct((WAVES * CHUNK, K), BF16),
        ],
        scratch_shapes=[
            pltpu.VMEM((TOP + PACKED, K), BF16),
            pltpu.VMEM((WAVES * LINE, K), F32),
        ],
        compiler_params=params(),
        cost_estimate=pl.CostEstimate(
            flops=2 * 10 * 192 * 640 * 128, bytes_accessed=5000000, transcendentals=0
        ),
        name="inverse_sums",
    )(own, block, straight, everything)


def finish_kernel(
    got_ref, sign_ref, table_ref, out_ref, table, made, rows, left, loads, stores
):
    parts, _, _, block = table.shape
    lines = ROWS * FIELDS

    def load(part):
        at = pl.ds(pl.multiple_of(part * block, 128), block)
        return pltpu.make_async_copy(
            table_ref.at[:, :, at], table.at[part], loads.at[part]
        )

    def store(part, half):
        at = pl.ds(pl.multiple_of(half * HALF + part * block, 128), block)
        return pltpu.make_async_copy(
            made.at[part, half], out_ref.at[:, at], stores.at[part, half]
        )

    for part in range(parts):
        load(part).start()
    loosen(got_ref, rows)
    sign = sign_ref[...]
    for li in range(ROWS):
        values = jnp.concatenate(
            [
                rows[pl.ds(slot * ROWS + li, WAVES, stride=LINE), :]
                for slot in range(SLOTS)
            ],
            axis=0,
        )
        turned = values.T
        for half, one in enumerate((turned, turned * sign)):
            at = slice(half * lines + li * FIELDS, half * lines + (li + 1) * FIELDS)
            left[at, :TOP] = one[:FIELDS].astype(BF16)
            left[at, TOP:] = one[FIELDS:].astype(BF16)

    @pl.loop(0, parts)
    def _(part):
        load(part).wait()
        right = table[part].reshape(2 * TOP, block)
        both = jnp.dot(left[...], right, preferred_element_type=F32).astype(BF16)
        for half in range(2):
            made[part, half] = both[half * lines : (half + 1) * lines]
            store(part, half).start()
    for part in range(parts):
        for half in range(2):
            store(part, half).wait()


def finish(got, sign, table):
    parts = 5
    block = HALF // parts
    return pl.pallas_call(
        finish_kernel,
        in_specs=[
            pl.BlockSpec(memory_space=pltpu.VMEM),
            pl.BlockSpec(memory_space=pltpu.VMEM),
            pl.BlockSpec(memory_space=pl.ANY),
        ],
        out_specs=pl.BlockSpec(memory_space=pl.ANY),
        out_shape=jax.ShapeDtypeStruct((ROWS * FIELDS, NLON), BF16),
        scratch_shapes=[
            pltpu.VMEM((parts, 2, TOP, block), BF16),
            pltpu.VMEM((parts, 2, ROWS * FIELDS, block), BF16),
            pltpu.VMEM((WAVES * LINE, K), F32),
            pltpu.VMEM((2 * ROWS * FIELDS, 2 * TOP), BF16),
            pltpu.SemaphoreType.DMA((parts,)),
            pltpu.SemaphoreType.DMA((parts, 2)),
        ],
        compiler_params=pltpu.CompilerParams(vmem_limit_bytes=MIDDLE),
        cost_estimate=pl.CostEstimate(
            flops=2 * 192 * 2560 * 1280, bytes_accessed=6000000, transcendentals=0
        ),
        name="finish_rows",
    )(got, sign, table)


def coupling_matrix(couple_div, couple_temp):
    zero = jnp.zeros_like(couple_div)
    one = jnp.block([[zero, couple_temp.T], [couple_div.T, zero]])
    none = jnp.zeros_like(one)
    return jnp.block([[one, none], [none, one]])


def body(grid_in, legendre, wave_order, block_order, couple_div, couple_temp):
    lat = lax.axis_index("lat")
    wave = lax.axis_index("wave")
    send = forward(wave_order, grid_in.reshape(ROWS * FIELDS, NLON))
    swap = functools.partial(lax.all_to_all, split_axis=0, concat_axis=0, tiled=True)
    got = swap(send.reshape(WAVES, CHUNK, K), "wave")
    own = lax.dynamic_slice_in_dim(wave_order, wave * SLOTS, SLOTS)
    block = lax.dynamic_slice_in_dim(block_order, lat, 1)
    straight, turned = basis(own, legendre)
    waves = wave_order.reshape(WAVES, SLOTS).T.reshape(TOP)
    sign = (1 - 2 * (waves & 1)).astype(F32).reshape(1, TOP)
    table = inverse_table(jnp.broadcast_to(waves.astype(F32)[:, None], (TOP, 128)))
    matrix = coupling_matrix(couple_div, couple_temp)
    turned, straight, table, sign, matrix, block, own, lat = lax.optimization_barrier(
        (turned, straight, table, sign, matrix, block, own, lat.reshape(1))
    )
    packed = partial_sums(own, turned, got.reshape(WAVES * CHUNK, K))
    parts = swap(packed.reshape(GROUPS, SHARE, K), "lat")
    spectral = couple(own, lat, parts, matrix)
    everything = lax.all_gather(spectral, "lat", axis=0, tiled=True)
    spectral_out, send = inverse(own, block, straight, everything)
    got = swap(send.reshape(WAVES, CHUNK, K), "wave")
    grid_out = finish(got.reshape(WAVES * CHUNK, K), sign, table)
    return spectral_out.transpose(1, 0, 2), grid_out.reshape(ROWS, FIELDS, NLON)


def solution(mesh):
    placed = (P(("lat", "wave"), None, None), P("wave", "lat", None), P(), P(), P(), P())
    return jax.shard_map(
        body,
        mesh=mesh,
        in_specs=placed,
        out_specs=(P("lat", "wave", None), P(("lat", "wave"), None, None)),
        check_vma=False,
    )
```
